512 devices in a mesh: dp: 64 (over y, x, core), head: 8 (over z).
Axes of the slice: x: 4, y: 8, z: 8, core: 2. Of those that a mesh axis runs over, the one named last changes fastest.
Arguments:
- q_in: bfloat16 [65536, 3072], P(('dp', 'head')), may hold values from -8 to 8
- k_in: bfloat16 [65536, 512], P(('dp', 'head')), may hold values from -8 to 8
- v_in: bfloat16 [65536, 512], P(('dp', 'head')), may hold values from -6 to 6
- dout: bfloat16 [65536, 3072], P(('dp', 'head')), may hold values from -6 to 6
- swap_plan: int32 [3, 512], P(None, ('dp', 'head')), may hold values from 0 to 1, as said below
- doc_ids: int32 [64, 8], P('dp'), may hold values from 0 to 2, never falling along the last dimension, each value on 1 to 5 neighbouring positions
Outputs:
- out: bfloat16 [65536, 3072], P(('dp', 'head'))
- dq: bfloat16 [65536, 3072], P(('dp', 'head'))
- dk: bfloat16 [65536, 512], P(('dp', 'head'))
- dv: bfloat16 [65536, 512], P(('dp', 'head'))
The draws below stay inside these ranges and needn't reach their ends.
Inputs may be any that keep to these rules, and one draw needn't show every extreme that they name: swap_plan[r, s] equals swap_plan[r, partner] for the partner of slot s in round r, as defined in the reference program. `doc_ids`: each row never falls; every id 0 .. 2 appears in every row.
All inputs are finite; a program needn't handle non-finite values.
Results may differ from the reference program's by a relative error of at most 0.024.
Values may be sent and summed in bfloat16 or wider, within the bound.
A program may use at most 64 MiB of HBM per device.

```python
import math
import jax
import jax.numpy as jnp
import numpy as np
from jax import lax

Q_HEADS = 24
KV_HEADS = 4
HEAD_DIM = 128
TILE_ROWS = 128
ROUNDS = 3
GROUP_TILES = 8
ALL_TILES = 512
SEQ_LEN = 1024
TOKENS = 65536
DOC_COUNT = 3
DOC_MOST = 5
N_DP = 64


def draw_k_in(key, part):
    key = jax.random.fold_in(key, 7)
    base = jax.random.truncated_normal(key, -4.0, 4.0, (TOKENS, KV_HEADS, HEAD_DIM), jnp.float32)
    return base.reshape(TOKENS, KV_HEADS * HEAD_DIM).astype(jnp.bfloat16)


def draw_q_in(key, part):
    key = jax.random.fold_in(key, 9)
    base = jax.random.truncated_normal(key, -4.0, 4.0, (TOKENS, Q_HEADS, HEAD_DIM), jnp.float32)
    return base.reshape(TOKENS, Q_HEADS * HEAD_DIM).astype(jnp.bfloat16)


def draw_swap_plan(key, part):
    key = jax.random.fold_in(key, 3)
    coins = jax.random.randint(key, (ROUNDS, ALL_TILES), 0, 2)
    slots = jnp.arange(ALL_TILES, dtype=jnp.int32)
    groups = slots // GROUP_TILES
    group_total = ALL_TILES // GROUP_TILES
    picked = []
    for turn_index in range(ROUNDS):
        stride = group_total // 2 ** (turn_index + 1)
        partner = jnp.bitwise_xor(groups, stride) * GROUP_TILES + slots % GROUP_TILES
        lower = jnp.minimum(slots, partner)
        picked.append(coins[turn_index][lower])
    return jnp.stack(picked).astype(jnp.int32)


def steps_of(rng, extent, pieces, least, top_value):
    level = 1.0
    for axis_at, shards_of in pieces:
        draws = jax.random.uniform(jax.random.fold_in(jax.random.fold_in(rng, 6), axis_at), (shards_of,), jnp.float32, least / len(pieces), top_value / len(pieces))
        level = level * jnp.repeat(jnp.exp(draws), extent[axis_at] // shards_of).reshape((-1,) + (1,) * (len(extent) - 1 - axis_at))
    return level


def profile(amount, total, limit, slope):
    portions = [(1 << 20) // math.isqrt(rank ** slope) + 1 for rank in range(2, amount + 1)]
    spare, counts = total - limit - (amount - 1), [1] * (amount - 1)
    while spare > 0:
        free = [i for i in range(amount - 1) if counts[i] < limit]
        pool, left = sum([portions[i] for i in free]), spare
        for i in free:
            addition = min(limit - counts[i], max(1, left * portions[i] // pool), spare)
            counts[i] = counts[i] + addition
            spare = spare - addition
    return np.array([limit] + counts)


def uneven(key, count, total, limit, lean):
    if count == 2:
        one = jax.random.randint(key, (), max(1, total - limit), min(limit, total - 1) + 1)
        return jnp.stack([one, total - one])
    lengths = jnp.asarray(profile(count, total, limit, lean), jnp.int32)
    twos = (count - 1) // 2
    source_of, taker = lengths[1:1 + 2 * twos:2], lengths[2:2 + 2 * twos:2]
    margin = jnp.minimum(source_of - 1, limit - taker)
    shifted = jax.random.randint(jax.random.fold_in(key, 1), (twos,), 0, 1 << 20) % (margin + 1)
    lengths = lengths.at[1:1 + 2 * twos:2].set(source_of - shifted).at[2:2 + 2 * twos:2].set(taker + shifted)
    return lengths[jax.random.permutation(jax.random.fold_in(key, 2), count)]


def centred(own_key, extent, width, reach, split=(), kind=jnp.bfloat16):
    factor_of = steps_of(own_key, extent, split, -0.22, 0.18) if split else 1.0
    entries = jax.random.normal(own_key, extent, jnp.float32) * width * factor_of
    return jnp.minimum(jnp.maximum(entries, -reach), reach).astype(kind)


def setup_inputs(seed: int = 0) -> dict:
    key_list = jax.random.split(jax.random.key(seed), 7)
    return {
        "q_in": draw_q_in(jax.random.fold_in(key_list[6], 71), 0),
        "k_in": draw_k_in(jax.random.fold_in(key_list[6], 71), 0),
        "v_in": centred(key_list[2], (TOKENS, KV_HEADS * HEAD_DIM), 1.0, 6.0, ((0, 512),)),
        "dout": centred(key_list[3], (TOKENS, Q_HEADS * HEAD_DIM), 1.0, 6.0, ((0, 512),)),
        "swap_plan": draw_swap_plan(jax.random.fold_in(key_list[6], 71), 0),
        "doc_ids": jax.vmap(lambda own: jnp.searchsorted(jnp.cumsum(uneven(own, DOC_COUNT, GROUP_TILES, DOC_MOST, 2)), jnp.arange(GROUP_TILES), side="right"))(jax.random.split(key_list[5], N_DP)).reshape((N_DP, GROUP_TILES)).astype(jnp.int32),
    }


def arrangement(swap_plan):
    slots = jnp.arange(ALL_TILES, dtype=jnp.int32)
    groups = slots // GROUP_TILES
    order = slots
    for turn_index in range(ROUNDS):
        stride = N_DP // (2 ** (turn_index + 1))
        partner = (jnp.bitwise_xor(groups, stride) * GROUP_TILES + slots % GROUP_TILES).astype(jnp.int32)
        order = jnp.where(swap_plan[turn_index] == 1, order[partner], order)
    return order


def group_pass(items):
    query, keys, values, grad_out, docs = items
    per_kv = Q_HEADS // KV_HEADS
    scale = HEAD_DIM ** -0.5
    query_f = query.astype(jnp.float32).reshape(SEQ_LEN, KV_HEADS, per_kv, HEAD_DIM)
    grad_f = grad_out.astype(jnp.float32).reshape(SEQ_LEN, KV_HEADS, per_kv, HEAD_DIM)
    keys_f = keys.astype(jnp.float32).reshape(SEQ_LEN, KV_HEADS, HEAD_DIM)
    values_f = values.astype(jnp.float32).reshape(SEQ_LEN, KV_HEADS, HEAD_DIM)
    token_doc = jnp.repeat(docs, TILE_ROWS)
    position = jnp.arange(SEQ_LEN, dtype=jnp.int32)
    allowed = (token_doc[:, None] == token_doc[None, :]) & (position[None, :] <= position[:, None])
    scores = jnp.einsum("qngd,knd->ngqk", query_f, keys_f) * scale
    scores = jnp.where(allowed, scores, -jnp.inf)
    peak = jnp.max(scores, axis=-1, keepdims=True)
    total = jnp.sum(jnp.exp(scores - peak), axis=-1, keepdims=True)
    probs = jnp.exp(scores - (peak + jnp.log(total)))
    weights = probs.astype(jnp.bfloat16)
    weights_f = weights.astype(jnp.float32)
    out = jnp.einsum("ngqk,knd->qngd", weights_f, values_f).astype(jnp.bfloat16)
    delta = jnp.sum(grad_f * out.astype(jnp.float32), axis=-1)
    dprobs = jnp.einsum("qngd,knd->ngqk", grad_f, values_f)
    dscores = (probs * (dprobs - jnp.transpose(delta, (1, 2, 0))[..., None]) * scale).astype(jnp.bfloat16)
    dscores_f = dscores.astype(jnp.float32)
    grad_query = jnp.einsum("ngqk,knd->qngd", dscores_f, keys_f).astype(jnp.bfloat16)
    grad_keys = jnp.einsum("ngqk,qngd->knd", dscores_f, query_f).astype(jnp.bfloat16)
    grad_values = jnp.einsum("ngqk,qngd->knd", weights_f, grad_f).astype(jnp.bfloat16)
    return (out.reshape(SEQ_LEN, -1), grad_query.reshape(SEQ_LEN, -1),
            grad_keys.reshape(SEQ_LEN, -1), grad_values.reshape(SEQ_LEN, -1))


def reference(q_in, k_in, v_in, dout, swap_plan, doc_ids):
    order = arrangement(swap_plan)

    def balanced(array):
        return array.reshape(ALL_TILES, TILE_ROWS, -1)[order].reshape(N_DP, SEQ_LEN, -1)

    def restored(array):
        tiles = array.reshape(ALL_TILES, TILE_ROWS, -1)
        empty = jnp.zeros(tiles.shape, tiles.dtype)
        return empty.at[order].set(tiles).reshape(TOKENS, -1)

    out, grad_query, grad_keys, grad_values = lax.map(
        group_pass, (balanced(q_in), balanced(k_in), balanced(v_in), dout.reshape(N_DP, SEQ_LEN, -1), doc_ids))
    return out.reshape(TOKENS, -1), restored(grad_query), restored(grad_keys), restored(grad_values)
```

```python
import functools

import jax
import jax.numpy as jnp
from jax import lax
from jax.experimental import pallas as pl
from jax.experimental.pallas import tpu as pltpu
from jax.sharding import PartitionSpec as P

HD = 128
TILE = 128
NY = 8
NX = 4
NZ = 8
NH = 3
SLOTS = 5
SCALE = HD**-0.5
LOG2E = 1.4426950408889634
FAR = -1e30
MESH = pl.DeviceIdType.MESH
F32 = jnp.float32
BF16 = jnp.bfloat16


def exchange(tiles, masks, rounds):
    tiles = list(tiles)
    for r in rounds:
        stride = 4 >> r
        tiles = [jnp.where(masks[r][y], tiles[y ^ stride], tiles[y]) for y in range(NY)]
    return tiles


def kernel(
    swap_ref, docs_ref, q_ref, k_ref, v_ref, g_ref,
    out_ref, dq_ref, dk_ref, dv_ref,
    meta_src, meta, kv_raw, kv, kv_t, q_raw, q_bal, g_in,
    o_buf, dq_bal, dq_buf, acc, pair_out, pair_in, chain_out, chain_in, fin,
    meta_ss, meta_rs, kv_ss, kv_rs, q_ss, q_rs, g_ss, g_rs,
    kz_ss, kz_rs, kc_ss, kc_rs, o_ss, o_rs, dq_ss, dq_rs,
    pc_ss, pc_rs, cz_ss, cz_rs, f_ss, f_rs,
):
    dp = lax.axis_index("dp")
    z = lax.axis_index("head")
    y, x, c = dp // (2 * NX), (dp // 2) % NX, dp % 2
    own, other = y % 2, 1 - c
    kv_head = y // 2
    mate = dp + 1 - 2 * c

    def dp_of(yy, cc):
        return (yy * NX + x) * 2 + cc

    def move(src, dst, send_sem, recv_sem, target, here):
        @pl.when(jnp.logical_not(here))
        def _():
            pltpu.make_async_remote_copy(
                src, dst, send_sem, recv_sem, device_id=(target, z), device_id_type=MESH
            ).start()

        @pl.when(here)
        def _():
            pltpu.make_async_copy(src, dst, recv_sem).start()

    def wait(ref, sem):
        pltpu.make_async_copy(ref, ref, sem).wait()

    def wait_sent(ref, sem):
        @pl.when(own == c)
        def _():
            wait(ref.at[0 : NY - 1], sem)

        @pl.when(own != c)
        def _():
            wait(ref, sem)

    mine = docs_ref[0, z]
    meta_src[0:1, :] = jnp.zeros((1, HD), F32)
    for t in range(1, SLOTS):
        same = (docs_ref[0, jnp.maximum(z - t, 0)] == mine) & (z >= t)
        meta_src[t : t + 1, :] = jnp.full((1, HD), jnp.where(same, 0.0, FAR), F32)
    for r in range(3):
        meta_src[SLOTS + r : SLOTS + r + 1, :] = jnp.full((1, HD), swap_ref[r, 0].astype(F32), F32)

    barrier = pltpu.get_barrier_semaphore()
    me = y * 2 + c
    for step in range(1, 16):
        peer = lax.rem(me + step, 16)
        pl.semaphore_signal(barrier, inc=1, device_id=(dp_of(peer // 2, peer % 2), z), device_id_type=MESH)

    @pl.when(z < NZ - 1)
    def _():
        pl.semaphore_signal(barrier, inc=1, device_id=(dp, z + 1), device_id_type=MESH)

    @pl.when(z > 0)
    def _():
        pl.semaphore_signal(barrier, inc=1, device_id=(dp, z - 1), device_id_type=MESH)

    @pl.when((z > 0) & (z < NZ - 1))
    def _():
        pl.semaphore_wait(barrier, 17)

    @pl.when((z == 0) | (z == NZ - 1))
    def _():
        pl.semaphore_wait(barrier, 16)

    dests = []
    for i in range(4):
        for j in range(2):
            head, core = lax.rem(kv_head + i, 4), lax.rem(c + j, 2)
            to = 2 * head + c
            dests.append((head, core, to, (to == y) & (core == c)))
    for head, core, to, here in dests:
        move(meta_src, meta.at[y], meta_ss, meta_rs, dp_of(to, core), here)
    for head, core, to, here in dests:
        cols = pl.ds(pl.multiple_of(head * HD, HD), HD)

        @pl.when(core == 0)
        def _():
            move(k_ref.at[:, cols], kv_raw.at[y], kv_ss, kv_rs, dp_of(to, core), here)

        @pl.when(core == 1)
        def _():
            move(v_ref.at[:, cols], kv_raw.at[y], kv_ss, kv_rs, dp_of(to, core), here)

    for h in range(NH):
        for src, dst, ss, rs in ((q_ref, q_raw, q_ss, q_rs), (g_ref, g_in, g_ss, g_rs)):
            for head, core, to, here in dests:
                cols = pl.ds(pl.multiple_of((6 * head + 3 * core + h) * HD, HD), HD)
                move(src.at[:, cols], dst.at[h, y], ss.at[h], rs.at[h], dp_of(to, core), here)

    for t in range(1, SLOTS):

        @pl.when(z < t)
        def _():
            kv[:, :, t] = jnp.zeros((2, NY, TILE, HD), BF16)

    @pl.when(z == NZ - 1)
    def _():
        chain_in[...] = jnp.zeros_like(chain_in)

    wait(meta, meta_rs)
    wait(kv_raw, kv_rs)

    def masks_of():
        return [[meta[y_, SLOTS + r : SLOTS + r + 1, :] > 0.5 for y_ in range(NY)] for r in range(3)]

    def place(read, write, rounds):
        masks = masks_of()

        def rows(i, carry):
            at = pl.ds(pl.multiple_of(i * 16, 16), 16)
            tiles = exchange([read(y_, at) for y_ in range(NY)], masks, rounds)
            for y_ in range(NY):
                write(y_, at, tiles[y_].astype(BF16))
            return carry

        lax.fori_loop(0, TILE // 16, rows, 0)

    def write_kv(y_, at, value):
        kv[c, y_, 0, at, :] = value

    place(lambda y_, at: kv_raw[y_, at, :].astype(F32), write_kv, (0, 1, 2))

    for t in range(SLOTS):
        if t > 0:

            @pl.when(z >= t)
            def _():
                wait(kv.at[0, :, t], kz_rs.at[t - 1])

        @pl.when(z >= t)
        def _():
            pltpu.make_async_remote_copy(
                kv.at[c, :, t], kv.at[c, :, t], kc_ss.at[t], kc_rs.at[t],
                device_id=(mate, z), device_id_type=MESH,
            ).start()

        if t < SLOTS - 1:

            @pl.when((z >= t) & (z < NZ - 1))
            def _():
                pltpu.make_async_remote_copy(
                    kv.at[c, :, t], kv.at[c, :, t + 1], kz_ss.at[t], kz_rs.at[t],
                    device_id=(dp, z + 1), device_id_type=MESH,
                ).start()

    for t in range(SLOTS):

        @pl.when(z >= t)
        def _():
            wait(kv.at[0, :, t], kc_rs.at[t])

    row = lax.broadcasted_iota(jnp.int32, (TILE, HD), 0)
    col = lax.broadcasted_iota(jnp.int32, (TILE, HD), 1)

    def attend(heads, first):
        lanes = len(heads) * TILE
        h0 = heads[0]

        def group(y_, carry):
            keys = kv[0, y_].reshape(SLOTS * TILE, HD)
            values = kv[1, y_].reshape(SLOTS * TILE, HD)
            if first:
                kv_t[0, y_] = keys.T
                kv_t[1, y_] = values.T
            query = q_bal[h0 : h0 + len(heads), y_].reshape(lanes, HD)
            grad = g_in[h0 : h0 + len(heads), y_].reshape(lanes, HD)
            nt = (((1,), (1,)), ((), ()))
            scores = lax.dot_general(keys, query, nt, preferred_element_type=F32) * (SCALE * LOG2E)
            parts = []
            for t in range(SLOTS):
                part = scores[t * TILE : (t + 1) * TILE]
                if t == 0:
                    causal = jnp.concatenate([row <= col] * len(heads), axis=1) if len(heads) > 1 else row <= col
                    part = jnp.where(causal, part, FAR)
                else:
                    bias = meta[y_, t : t + 1, :]
                    bias = jnp.concatenate([bias] * len(heads), axis=1) if len(heads) > 1 else bias
                    part = part + bias
                parts.append(part)
            scores = jnp.concatenate(parts, axis=0)
            peak = jnp.max(scores, axis=0, keepdims=True)
            probs = jnp.exp2(scores - peak)
            probs = probs * (1.0 / jnp.sum(probs, axis=0, keepdims=True))
            weights = probs.astype(BF16)
            out_t = jnp.dot(kv_t[1, y_], weights, preferred_element_type=F32)
            o_buf[h0 : h0 + len(heads), y_] = out_t.T.astype(BF16).reshape(len(heads), TILE, HD)
            dprobs = lax.dot_general(values, grad, nt, preferred_element_type=F32)
            delta = jnp.sum(probs * dprobs, axis=0, keepdims=True)
            dscores = (probs * (dprobs - delta)).astype(BF16)
            dq_t = jnp.dot(kv_t[0, y_], dscores, preferred_element_type=F32) * SCALE
            dq_bal[h0 : h0 + len(heads), y_] = dq_t.T.astype(BF16).reshape(len(heads), TILE, HD)
            dk = jnp.dot(dscores, query, preferred_element_type=F32).reshape(SLOTS, TILE, HD)
            dv = jnp.dot(weights, grad, preferred_element_type=F32).reshape(SLOTS, TILE, HD)
            if first:
                acc[0, y_] = dk
                acc[1, y_] = dv
            else:
                acc[0, y_] += dk
                acc[1, y_] += dv
            return carry

        for h in heads:
            wait(q_raw.at[h], q_rs.at[h])

            def write_q(y_, at, value, h=h):
                q_bal[h, y_, at, :] = value

            place(lambda y_, at, h=h: q_raw[h, y_, at, :].astype(F32), write_q, (0, 1, 2))
        for h in heads:
            wait(g_in.at[h], g_rs.at[h])
        lax.fori_loop(0, NY, group, 0)

        for h in heads:

            def write_dq(y_, at, value, h=h):
                dq_buf[h, y_, at, :] = value

            place(lambda y_, at, h=h: dq_bal[h, y_, at, :].astype(F32), write_dq, (2, 1, 0))
            cols = pl.ds(pl.multiple_of((6 * kv_head + 3 * c + h) * HD, HD), HD)
            for i in range(NY):
                to = lax.rem(y + i, NY)
                here = (to == y) & (own == c)
                move(o_buf.at[h, to], out_ref.at[:, cols], o_ss.at[h], o_rs, dp_of(to, own), here)
                move(dq_buf.at[h, to], dq_ref.at[:, cols], dq_ss.at[h], dq_rs, dp_of(to, own), here)

    attend((0, 1), True)
    attend((2,), False)

    for t in reversed(range(SLOTS)):

        @pl.when(z >= t)
        def _():
            pair_out[t] = acc[other, :, t].astype(BF16)
            pltpu.make_async_remote_copy(
                pair_out.at[t], pair_in.at[t], pc_ss.at[t], pc_rs.at[t],
                device_id=(mate, z), device_id_type=MESH,
            ).start()

    for t in reversed(range(1, SLOTS)):

        @pl.when(z >= t)
        def _():
            wait(pair_in.at[t], pc_rs.at[t])
            if t < SLOTS - 1:

                @pl.when(z < NZ - 1)
                def _():
                    wait(chain_in.at[t], cz_rs.at[t])

                chain_out[t - 1] = (acc[c, :, t] + pair_in[t].astype(F32) + chain_in[t].astype(F32)).astype(BF16)
            else:
                chain_out[t - 1] = (acc[c, :, t] + pair_in[t].astype(F32)).astype(BF16)
            pltpu.make_async_remote_copy(
                chain_out.at[t - 1], chain_in.at[t - 1], cz_ss.at[t - 1], cz_rs.at[t - 1],
                device_id=(dp, z - 1), device_id_type=MESH,
            ).start()

    wait(pair_in.at[0], pc_rs.at[0])

    @pl.when(z < NZ - 1)
    def _():
        wait(chain_in.at[0], cz_rs.at[0])

    factor = jnp.where(c == 0, SCALE, 1.0).astype(F32)

    def read_total(y_, at):
        total = acc[c, y_, 0, at, :] + pair_in[0, y_, at, :].astype(F32) + chain_in[0, y_, at, :].astype(F32)
        return total * factor

    def write_total(y_, at, value):
        fin[y_, at, :] = value

    place(read_total, write_total, (2, 1, 0))
    cols = pl.ds(pl.multiple_of(kv_head * HD, HD), HD)
    for i in range(NY):
        to = lax.rem(y + i, NY)
        here = (to == y) & (own == c)

        @pl.when(c == 0)
        def _():
            move(fin.at[to], dk_ref.at[:, cols], f_ss, f_rs.at[0], dp_of(to, own), here)

        @pl.when(c == 1)
        def _():
            move(fin.at[to], dv_ref.at[:, cols], f_ss, f_rs.at[1], dp_of(to, own), here)

    wait(out_ref, o_rs)
    wait(dq_ref, dq_rs)
    wait(dk_ref, f_rs.at[0])
    wait(dv_ref, f_rs.at[1])
    wait_sent(meta, meta_ss)
    wait_sent(kv_raw, kv_ss)
    wait_sent(fin, f_ss)
    for h in range(NH):
        wait_sent(q_raw.at[h], q_ss.at[h])
        wait_sent(g_in.at[h], g_ss.at[h])
        wait_sent(o_buf.at[h], o_ss.at[h])
        wait_sent(dq_buf.at[h], dq_ss.at[h])
    for t in range(SLOTS):

        @pl.when(z >= t)
        def _():
            wait(kv.at[0, :, t], kc_ss.at[t])
            wait(pair_out.at[t], pc_ss.at[t])

    for t in range(SLOTS - 1):

        @pl.when((z >= t) & (z < NZ - 1))
        def _():
            wait(kv.at[0, :, t], kz_ss.at[t])

        @pl.when(z >= t + 1)
        def _():
            wait(chain_out.at[t], cz_ss.at[t])


def on_device(q_in, k_in, v_in, dout, swap_plan, doc_ids):
    tile = (TILE, HD)
    dma = pltpu.SemaphoreType.DMA
    hbm, smem = pl.BlockSpec(memory_space=pl.ANY), pl.BlockSpec(memory_space=pltpu.SMEM)
    return pl.pallas_call(
        kernel,
        out_shape=[jax.ShapeDtypeStruct(a.shape, BF16) for a in (dout, q_in, k_in, v_in)],
        in_specs=[smem, smem, hbm, hbm, hbm, hbm],
        out_specs=[hbm] * 4,
        scratch_shapes=[
            pltpu.VMEM((8, HD), F32),
            pltpu.VMEM((NY, 8, HD), F32),
            pltpu.VMEM((NY, *tile), BF16),
            pltpu.VMEM((2, NY, SLOTS, *tile), BF16),
            pltpu.VMEM((2, NY, HD, SLOTS * TILE), BF16),
            pltpu.VMEM((NH, NY, *tile), BF16),
            pltpu.VMEM((NH, NY, *tile), BF16),
            pltpu.VMEM((NH, NY, *tile), BF16),
            pltpu.VMEM((NH, NY, *tile), BF16),
            pltpu.VMEM((NH, NY, *tile), BF16),
            pltpu.VMEM((NH, NY, *tile), BF16),
            pltpu.VMEM((2, NY, SLOTS, *tile), F32),
            pltpu.VMEM((SLOTS, NY, *tile), BF16),
            pltpu.VMEM((SLOTS, NY, *tile), BF16),
            pltpu.VMEM((SLOTS - 1, NY, *tile), BF16),
            pltpu.VMEM((SLOTS - 1, NY, *tile), BF16),
            pltpu.VMEM((NY, *tile), BF16),
            dma, dma, dma, dma,
            dma((NH,)), dma((NH,)), dma((NH,)), dma((NH,)),
            dma((SLOTS - 1,)), dma((SLOTS - 1,)), dma((SLOTS,)), dma((SLOTS,)),
            dma((NH,)), dma, dma((NH,)), dma,
            dma((SLOTS,)), dma((SLOTS,)), dma((SLOTS - 1,)), dma((SLOTS - 1,)),
            dma, dma((2,)),
        ],
        compiler_params=pltpu.CompilerParams(
            collective_id=0, has_side_effects=True, vmem_limit_bytes=48 << 20
        ),
    )(swap_plan, doc_ids, q_in, k_in, v_in, dout)


def solution(mesh):
    rows = P(("dp", "head"), None)
    return jax.shard_map(
        on_device,
        mesh=mesh,
        in_specs=(rows, rows, rows, rows, P(None, ("dp", "head")), P("dp", None)),
        out_specs=(rows, rows, rows, rows),
        check_vma=False,
    )
```

```python
import functools

import jax
import jax.numpy as jnp
from jax import lax
from jax.experimental import pallas as pl
from jax.experimental.pallas import tpu as pltpu
from jax.sharding import PartitionSpec as P

HD = 128
TILE = 128
NY = 8
NX = 4
NZ = 8
NH = 3
HALF = NY // 2
SLOTS = 5
SCALE = HD**-0.5
LOG2E = 1.4426950408889634
FAR = -1e30
MESH = pl.DeviceIdType.MESH
UPFRONT = ((0, 1, 2), (), ())
F32 = jnp.float32
BF16 = jnp.bfloat16


ORDER = (4, 3, 5, 2, 6, 1, 7, 0)


def exchange(tiles, masks, rounds):
    tiles = list(tiles)
    for r in rounds:
        stride = 4 >> r
        tiles = [jnp.where(masks[r][y], tiles[y ^ stride], tiles[y]) for y in range(NY)]
    return tiles


def kernel(
    swap_ref, docs_ref, q_ref, k_ref, v_ref, g_ref,
    out_ref, dq_ref, dk_ref, dv_ref,
    meta_src, meta, kv_raw, kv, kv_t, q_raw, q_bal, g_in,
    o_buf, dq_bal, dq_buf, acc, pair_out, pair_in, chain_out, chain_in, fin,
    meta_ss, meta_rs, kv_ss, kv_rs, q_ss, q_rs, g_ss, g_rs,
    kz_ss, kz_rs, kc_ss, kc_rs, o_ss, o_rs, dq_ss, dq_rs,
    pc_ss, pc_rs, cz_ss, cz_rs, f_ss, f_rs,
):
    dp = lax.axis_index("dp")
    z = lax.axis_index("head")
    y, x, c = dp // (2 * NX), (dp // 2) % NX, dp % 2
    own, other = y % 2, 1 - c
    kv_head = y // 2
    mate = dp + 1 - 2 * c

    def dp_of(yy, cc):
        return (yy * NX + x) * 2 + cc

    def move(src, dst, send_sem, recv_sem, target, here):
        @pl.when(jnp.logical_not(here))
        def _():
            pltpu.make_async_remote_copy(
                src, dst, send_sem, recv_sem, device_id=(target, z), device_id_type=MESH
            ).start()

        @pl.when(here)
        def _():
            pltpu.make_async_copy(src, dst, recv_sem).start()

    def wait(ref, sem):
        pltpu.make_async_copy(ref, ref, sem).wait()

    def wait_sent(ref, sem):
        @pl.when(own == c)
        def _():
            wait(ref.at[0 : NY - 1], sem)

        @pl.when(own != c)
        def _():
            wait(ref, sem)

    mine = docs_ref[0, z]
    meta_src[0:1, :] = jnp.zeros((1, HD), F32)
    for t in range(1, SLOTS):
        same = (docs_ref[0, jnp.maximum(z - t, 0)] == mine) & (z >= t)
        meta_src[t : t + 1, :] = jnp.full((1, HD), jnp.where(same, 0.0, FAR), F32)
    for r in range(3):
        meta_src[SLOTS + r : SLOTS + r + 1, :] = jnp.full((1, HD), swap_ref[0, r].astype(F32), F32)

    barrier = pltpu.get_barrier_semaphore()
    me = y * 2 + c
    for step in range(1, 16):
        peer = lax.rem(me + step, 16)
        pl.semaphore_signal(barrier, inc=1, device_id=(dp_of(peer // 2, peer % 2), z), device_id_type=MESH)

    @pl.when(z < NZ - 1)
    def _():
        pl.semaphore_signal(barrier, inc=1, device_id=(dp, z + 1), device_id_type=MESH)

    @pl.when(z > 0)
    def _():
        pl.semaphore_signal(barrier, inc=1, device_id=(dp, z - 1), device_id_type=MESH)

    @pl.when((z > 0) & (z < NZ - 1))
    def _():
        pl.semaphore_wait(barrier, 17)

    @pl.when((z == 0) | (z == NZ - 1))
    def _():
        pl.semaphore_wait(barrier, 16)

    dests = []
    for i in (2, 1, 3, 0):
        for j in range(2):
            head, core = lax.rem(kv_head + i, 4), lax.rem(c + j, 2)
            to = 2 * head + c
            dests.append((head, core, to, (to == y) & (core == c)))
    for head, core, to, here in dests:
        move(meta_src, meta.at[y], meta_ss, meta_rs, dp_of(to, core), here)
    for head, core, to, here in dests:
        cols = pl.ds(pl.multiple_of(head * HD, HD), HD)

        @pl.when(core == 0)
        def _():
            move(k_ref.at[:, cols], kv_raw.at[y], kv_ss, kv_rs, dp_of(to, core), here)

        @pl.when(core == 1)
        def _():
            move(v_ref.at[:, cols], kv_raw.at[y], kv_ss, kv_rs, dp_of(to, core), here)

    def send_heads(h):
        for src, dst, ss, rs in ((q_ref, q_raw, q_ss, q_rs), (g_ref, g_in, g_ss, g_rs)):
            for head, core, to, here in dests:
                cols = pl.ds(pl.multiple_of((6 * head + 3 * core + h) * HD, HD), HD)
                move(src.at[:, cols], dst.at[h, y], ss.at[h], rs.at[h], dp_of(to, core), here)

    for h in UPFRONT[0]:
        send_heads(h)

    for t in range(1, SLOTS):

        @pl.when(z < t)
        def _():
            kv[:, :, t] = jnp.zeros((2, NY, TILE, HD), BF16)

    @pl.when(z == NZ - 1)
    def _():
        chain_in[...] = jnp.zeros_like(chain_in)

    wait(meta, meta_rs)
    wait(kv_raw, kv_rs)

    def masks_of():
        return [[meta[y_, SLOTS + r : SLOTS + r + 1, :] > 0.5 for y_ in range(NY)] for r in range(3)]

    def place(read, write, rounds):
        masks = masks_of()

        def rows(i, carry):
            at = pl.ds(pl.multiple_of(i * 16, 16), 16)
            tiles = exchange([read(y_, at) for y_ in range(NY)], masks, rounds)
            for y_ in range(NY):
                write(y_, at, tiles[y_].astype(BF16))
            return carry

        lax.fori_loop(0, TILE // 16, rows, 0)

    def write_kv(y_, at, value):
        kv[c, y_, 0, at, :] = value

    place(lambda y_, at: kv_raw[y_, at, :].astype(F32), write_kv, (0, 1, 2))

    halves = [pl.ds(half * HALF, HALF) for half in range(2)]
    for t in range(SLOTS):
        for half in range(2):
            tiles = halves[half]
            if t > 0:

                @pl.when(z >= t)
                def _():
                    wait(kv.at[0, tiles, t], kz_rs.at[t - 1, half])

            @pl.when(z >= t)
            def _():
                pltpu.make_async_remote_copy(
                    kv.at[c, tiles, t], kv.at[c, tiles, t], kc_ss.at[t, half], kc_rs.at[t, half],
                    device_id=(mate, z), device_id_type=MESH,
                ).start()

            if t < SLOTS - 1:

                @pl.when((z >= t) & (z < NZ - 1))
                def _():
                    pltpu.make_async_remote_copy(
                        kv.at[c, tiles, t], kv.at[c, tiles, t + 1], kz_ss.at[t, half], kz_rs.at[t, half],
                        device_id=(dp, z + 1), device_id_type=MESH,
                    ).start()

        if t in (0, 1):
            for h in UPFRONT[t + 1]:
                send_heads(h)

    for t in range(SLOTS):
        for half in range(2):

            @pl.when(z >= t)
            def _():
                wait(kv.at[0, halves[half], t], kc_rs.at[t, half])

    def attend(heads, first, last):
        n = len(heads)
        lanes = n * TILE
        h0, h1 = heads[0], heads[-1] + 1
        nt = (((1,), (1,)), ((), ()))
        row = lax.broadcasted_iota(jnp.int32, (TILE, lanes), 0)
        col = lax.rem(lax.broadcasted_iota(jnp.int32, (TILE, lanes), 1), TILE)

        def group(i, carry):
            step = (i + 1) // 2
            y_ = lax.rem(y + 2 * NY + (HALF - step) * (2 * lax.rem(i, 2) - 1), NY)
            keys = kv[0, y_].reshape(SLOTS * TILE, HD)
            values = kv[1, y_].reshape(SLOTS * TILE, HD)
            if first:
                kv_t[0, y_] = keys.T
                kv_t[1, y_] = values.T
            query = q_bal[h0:h1, y_].reshape(lanes, HD)
            grad = g_in[h0:h1, y_].reshape(lanes, HD)
            scores = lax.dot_general(keys, query, nt, preferred_element_type=F32)
            dprobs = lax.dot_general(values, grad, nt, preferred_element_type=F32)
            parts = [scores[t * TILE : (t + 1) * TILE] for t in range(SLOTS)]
            parts[0] = jnp.where(row <= col, parts[0], FAR)
            bias = [jnp.concatenate([meta[y_, t : t + 1, :]] * n, axis=1) for t in range(SLOTS)]
            peaks = [jnp.max(parts[t], axis=0, keepdims=True) + bias[t] for t in range(SLOTS)]
            peak = functools.reduce(jnp.maximum, peaks)
            parts = [jnp.exp2((parts[t] - (peak - bias[t])) * (SCALE * LOG2E)) for t in range(SLOTS)]
            total = functools.reduce(jnp.add, [jnp.sum(part, axis=0, keepdims=True) for part in parts])
            inverse = 1.0 / total
            probs = jnp.concatenate([part * inverse for part in parts], axis=0)
            weights = probs.astype(BF16)
            delta = jnp.sum(probs * dprobs, axis=0, keepdims=True)
            dscores = (probs * (dprobs - delta)).astype(BF16)
            out_t = jnp.dot(kv_t[1, y_], weights, preferred_element_type=F32)
            o_buf[h0:h1, y_] = out_t.T.astype(BF16).reshape(n, TILE, HD)
            dq_t = jnp.dot(kv_t[0, y_], dscores, preferred_element_type=F32) * SCALE
            dq_bal[h0:h1, y_] = dq_t.T.astype(BF16).reshape(n, TILE, HD)
            dk = jnp.dot(dscores, query, preferred_element_type=F32).reshape(SLOTS, TILE, HD)
            dv = jnp.dot(weights, grad, preferred_element_type=F32).reshape(SLOTS, TILE, HD)
            if first:
                acc[0, i] = dk
                acc[1, i] = dv
            else:
                acc[0, i] += dk
                acc[1, i] += dv
            here = (y_ == y) & (own == c)
            for h in heads:
                cols = pl.ds(pl.multiple_of((6 * kv_head + 3 * c + h) * HD, HD), HD)
                move(o_buf.at[h, y_], out_ref.at[:, cols], o_ss.at[h], o_rs, dp_of(y_, own), here)
            if last:
                pair_out[i] = acc[other, i].astype(BF16)
                half = i // HALF
                pltpu.make_async_remote_copy(
                    pair_out.at[i], pair_in.at[i], pc_ss.at[half], pc_rs.at[half],
                    device_id=(mate, z), device_id_type=MESH,
                ).start()
            return carry

        for h in heads:
            wait(q_raw.at[h], q_rs.at[h])

            def write_q(y_, at, value, h=h):
                q_bal[h, y_, at, :] = value

            place(lambda y_, at, h=h: q_raw[h, y_, at, :].astype(F32), write_q, (0, 1, 2))
        for h in heads:
            wait(g_in.at[h], g_rs.at[h])
        lax.fori_loop(0, NY - 2 if last else NY, group, 0, unroll=2)
        if last:
            chain_step(SLOTS - 1, 0)
            lax.fori_loop(NY - 2, NY, group, 0, unroll=2)

    def send_dq(heads):
        for h in heads:

            def write_dq(y_, at, value, h=h):
                dq_buf[h, y_, at, :] = value

            place(lambda y_, at, h=h: dq_bal[h, y_, at, :].astype(F32), write_dq, (2, 1, 0))
            cols = pl.ds(pl.multiple_of((6 * kv_head + 3 * c + h) * HD, HD), HD)
            for i in ORDER:
                to = lax.rem(y + i, NY)
                here = (to == y) & (own == c)
                move(dq_buf.at[h, to], dq_ref.at[:, cols], dq_ss.at[h], dq_rs, dp_of(to, own), here)

    attend((0, 1), True, False)
    send_dq((0, 1))

    def chain_step(t, half):
        tiles = halves[half]
        if t == SLOTS - 1:
            wait(pair_in.at[tiles], pc_rs.at[half])

        @pl.when(z >= t)
        def _():
            if t < SLOTS - 1:

                @pl.when(z < NZ - 1)
                def _():
                    wait(chain_in.at[t, tiles], cz_rs.at[t, half])

            total = acc[c, tiles, t] + pair_in[tiles, t].astype(F32)
            if t < SLOTS - 1:
                total = total + chain_in[t, tiles].astype(F32)
            chain_out[t - 1, tiles] = total.astype(BF16)
            pltpu.make_async_remote_copy(
                chain_out.at[t - 1, tiles], chain_in.at[t - 1, tiles],
                cz_ss.at[t - 1, half], cz_rs.at[t - 1, half],
                device_id=(dp, z - 1), device_id_type=MESH,
            ).start()

    attend((2,), False, True)
    chain_step(SLOTS - 1, 1)
    send_dq((2,))
    for t in reversed(range(1, SLOTS - 1)):
        for half in range(2):
            chain_step(t, half)


    @pl.when(z < NZ - 1)
    def _():
        for half in range(2):
            wait(chain_in.at[0, halves[half]], cz_rs.at[0, half])

    factor = jnp.where(c == 0, SCALE, 1.0).astype(F32)

    def read_total(y_, at):
        d = lax.rem(y_ - y + NY, NY)
        i = (d // HALF) * (2 * (d - HALF)) + (1 - d // HALF) * (NY - 1 - 2 * d)
        total = acc[c, i, 0, at, :] + pair_in[i, 0, at, :].astype(F32) + chain_in[0, i, at, :].astype(F32)
        return total * factor

    def write_total(y_, at, value):
        fin[y_, at, :] = value

    place(read_total, write_total, (2, 1, 0))
    cols = pl.ds(pl.multiple_of(kv_head * HD, HD), HD)
    for i in ORDER:
        to = lax.rem(y + i, NY)
        here = (to == y) & (own == c)

        @pl.when(c == 0)
        def _():
            move(fin.at[to], dk_ref.at[:, cols], f_ss, f_rs.at[0], dp_of(to, own), here)

        @pl.when(c == 1)
        def _():
            move(fin.at[to], dv_ref.at[:, cols], f_ss, f_rs.at[1], dp_of(to, own), here)

    wait(out_ref, o_rs)
    wait(dq_ref, dq_rs)
    wait(dk_ref, f_rs.at[0])
    wait(dv_ref, f_rs.at[1])
    wait_sent(meta, meta_ss)
    wait_sent(kv_raw, kv_ss)
    wait_sent(fin, f_ss)
    for h in range(NH):
        wait_sent(q_raw.at[h], q_ss.at[h])
        wait_sent(g_in.at[h], g_ss.at[h])
        wait_sent(o_buf.at[h], o_ss.at[h])
        wait_sent(dq_buf.at[h], dq_ss.at[h])
    for half in range(2):
        tiles = halves[half]
        wait(pair_out.at[tiles], pc_ss.at[half])
        for t in range(SLOTS):

            @pl.when(z >= t)
            def _():
                wait(kv.at[0, tiles, t], kc_ss.at[t, half])

        for t in range(SLOTS - 1):

            @pl.when((z >= t) & (z < NZ - 1))
            def _():
                wait(kv.at[0, tiles, t], kz_ss.at[t, half])

            @pl.when(z >= t + 1)
            def _():
                wait(chain_out.at[t, tiles], cz_ss.at[t, half])


PIECES = 1


def hand_over(*refs):
    ins, outs, bufs, (read_sems, write_sems) = refs[0:4], refs[4:8], refs[8:12], refs[12:]
    pieces = [(a, pl.ds(p * (TILE // PIECES), TILE // PIECES)) for p in range(PIECES) for a in range(4)]
    reads = [pltpu.make_async_copy(ins[a].at[r], bufs[a].at[r], read_sems.at[i]) for i, (a, r) in enumerate(pieces)]
    writes = [pltpu.make_async_copy(bufs[a].at[r], outs[a].at[r], write_sems.at[i]) for i, (a, r) in enumerate(pieces)]
    for copy in reads:
        copy.start()
    for read, write in zip(reads, writes):
        read.wait()
        write.start()
    for copy in writes:
        copy.wait()


def on_device(q_in, k_in, v_in, dout, swap_plan, doc_ids):
    tile = (TILE, HD)
    dma = pltpu.SemaphoreType.DMA
    hbm, smem = pl.BlockSpec(memory_space=pl.ANY), pl.BlockSpec(memory_space=pltpu.SMEM)
    results = pl.pallas_call(
        kernel,
        out_shape=[jax.ShapeDtypeStruct(a.shape, BF16) for a in (dout, q_in, k_in, v_in)],
        in_specs=[smem, smem, hbm, hbm, hbm, hbm],
        out_specs=[hbm] * 4,
        scratch_shapes=[
            pltpu.VMEM((8, HD), F32),
            pltpu.VMEM((NY, 8, HD), F32),
            pltpu.VMEM((NY, *tile), BF16),
            pltpu.VMEM((2, NY, SLOTS, *tile), BF16),
            pltpu.VMEM((2, NY, HD, SLOTS * TILE), BF16),
            pltpu.VMEM((NH, NY, *tile), BF16),
            pltpu.VMEM((NH, NY, *tile), BF16),
            pltpu.VMEM((NH, NY, *tile), BF16),
            pltpu.VMEM((NH, NY, *tile), BF16),
            pltpu.VMEM((NH, NY, *tile), BF16),
            pltpu.VMEM((NH, NY, *tile), BF16),
            pltpu.VMEM((2, NY, SLOTS, *tile), F32),
            pltpu.VMEM((NY, SLOTS, *tile), BF16),
            pltpu.VMEM((NY, SLOTS, *tile), BF16),
            pltpu.VMEM((SLOTS - 1, NY, *tile), BF16),
            pltpu.VMEM((SLOTS - 1, NY, *tile), BF16),
            pltpu.VMEM((NY, *tile), BF16),
            dma, dma, dma, dma,
            dma((NH,)), dma((NH,)), dma((NH,)), dma((NH,)),
            dma((SLOTS - 1, 2)), dma((SLOTS - 1, 2)), dma((SLOTS, 2)), dma((SLOTS, 2)),
            dma((NH,)), dma, dma((NH,)), dma,
            dma((2,)), dma((2,)), dma((SLOTS - 1, 2)), dma((SLOTS - 1, 2)),
            dma, dma((2,)),
        ],
        compiler_params=pltpu.CompilerParams(
            collective_id=0, has_side_effects=True, vmem_limit_bytes=63 << 20
        ),
    )(swap_plan.reshape(1, 3), doc_ids, q_in, k_in, v_in, dout)
    return pl.pallas_call(
        hand_over,
        out_shape=[jax.ShapeDtypeStruct(a.shape, BF16) for a in results],
        in_specs=[hbm] * 4,
        out_specs=[hbm] * 4,
        scratch_shapes=[pltpu.VMEM(a.shape, BF16) for a in results] + [dma((4 * PIECES,)), dma((4 * PIECES,))],
    )(*results)


def solution(mesh):
    rows = P(("dp", "head"), None)
    return jax.shard_map(
        on_device,
        mesh=mesh,
        in_specs=(rows, rows, rows, rows, P(None, ("dp", "head")), P("dp", None)),
        out_specs=(rows, rows, rows, rows),
        check_vma=False,
    )
```

```python
import functools

import jax
import jax.numpy as jnp
from jax import lax
from jax.experimental import pallas as pl
from jax.experimental.pallas import tpu as pltpu
from jax.sharding import PartitionSpec as P

HD = 128
TILE = 128
NY = 8
NX = 4
NZ = 8
NH = 3
HALF = NY // 2
PARTS = 4
PART = NY // PARTS
SLOTS = 5
SCALE = HD**-0.5
LOG2E = 1.4426950408889634
FAR = -1e30
MESH = pl.DeviceIdType.MESH
UPFRONT = ((0, 1, 2), (), ())
F32 = jnp.float32
BF16 = jnp.bfloat16


ORDER = (4, 3, 5, 2, 6, 1, 7, 0)


def exchange(tiles, masks, rounds):
    tiles = list(tiles)
    for r in rounds:
        stride = 4 >> r
        tiles = [jnp.where(masks[r][y], tiles[y ^ stride], tiles[y]) for y in range(NY)]
    return tiles


def kernel(
    swap_ref, docs_ref, q_ref, k_ref, v_ref, g_ref,
    out_ref, dq_ref, dk_ref, dv_ref,
    meta_src, meta, kv_raw, kv, kv_t, q_raw, q_bal, g_in,
    o_buf, dq_bal, dq_buf, acc, pair_out, pair_in, chain_out, chain_in, fin,
    meta_ss, meta_rs, kv_ss, kv_rs, q_ss, q_rs, g_ss, g_rs,
    kz_ss, kz_rs, kc_ss, kc_rs, o_ss, o_rs, dq_ss, dq_rs,
    pc_ss, pc_rs, cz_ss, cz_rs, f_ss, f_rs,
):
    dp = lax.axis_index("dp")
    z = lax.axis_index("head")
    y, x, c = dp // (2 * NX), (dp // 2) % NX, dp % 2
    own, other = y % 2, 1 - c
    kv_head = y // 2
    mate = dp + 1 - 2 * c

    def dp_of(yy, cc):
        return (yy * NX + x) * 2 + cc

    def move(src, dst, send_sem, recv_sem, target, here):
        @pl.when(jnp.logical_not(here))
        def _():
            pltpu.make_async_remote_copy(
                src, dst, send_sem, recv_sem, device_id=(target, z), device_id_type=MESH
            ).start()

        @pl.when(here)
        def _():
            pltpu.make_async_copy(src, dst, recv_sem).start()

    def wait(ref, sem):
        pltpu.make_async_copy(ref, ref, sem).wait()

    def wait_sent(ref, sem):
        @pl.when(own == c)
        def _():
            wait(ref.at[0 : NY - 1], sem)

        @pl.when(own != c)
        def _():
            wait(ref, sem)

    barrier = pltpu.get_barrier_semaphore()
    me = y * 2 + c
    for step in range(1, 16):
        peer = lax.rem(me + step, 16)
        pl.semaphore_signal(barrier, inc=1, device_id=(dp_of(peer // 2, peer % 2), z), device_id_type=MESH)

    @pl.when(z < NZ - 1)
    def _():
        pl.semaphore_signal(barrier, inc=1, device_id=(dp, z + 1), device_id_type=MESH)

    @pl.when(z > 0)
    def _():
        pl.semaphore_signal(barrier, inc=1, device_id=(dp, z - 1), device_id_type=MESH)

    mine = docs_ref[0, z]
    meta_src[0:1, :] = jnp.zeros((1, HD), F32)
    for t in range(1, SLOTS):
        same = (docs_ref[0, jnp.maximum(z - t, 0)] == mine) & (z >= t)
        meta_src[t : t + 1, :] = jnp.full((1, HD), jnp.where(same, 0.0, FAR), F32)
    for r in range(3):
        meta_src[SLOTS + r : SLOTS + r + 1, :] = jnp.full((1, HD), swap_ref[0, r].astype(F32), F32)

    for t in range(1, SLOTS):

        @pl.when(z < t)
        def _():
            kv[:, :, t] = jnp.zeros((2, NY, TILE, HD), BF16)

    @pl.when(z == NZ - 1)
    def _():
        chain_in[...] = jnp.zeros_like(chain_in)

    @pl.when((z > 0) & (z < NZ - 1))
    def _():
        pl.semaphore_wait(barrier, 17)

    @pl.when((z == 0) | (z == NZ - 1))
    def _():
        pl.semaphore_wait(barrier, 16)

    dests = []
    for i in (2, 1, 3, 0):
        for j in range(2):
            head, core = lax.rem(kv_head + i, 4), lax.rem(c + j, 2)
            to = 2 * head + c
            dests.append((head, core, to, (to == y) & (core == c)))
    for head, core, to, here in dests:
        move(meta_src, meta.at[y], meta_ss, meta_rs, dp_of(to, core), here)
    for head, core, to, here in dests:
        cols = pl.ds(pl.multiple_of(head * HD, HD), HD)

        @pl.when(core == 0)
        def _():
            move(k_ref.at[:, cols], kv_raw.at[y], kv_ss, kv_rs, dp_of(to, core), here)

        @pl.when(core == 1)
        def _():
            move(v_ref.at[:, cols], kv_raw.at[y], kv_ss, kv_rs, dp_of(to, core), here)

    def send_heads(h):
        for src, dst, ss, rs in ((q_ref, q_raw, q_ss, q_rs), (g_ref, g_in, g_ss, g_rs)):
            for head, core, to, here in dests:
                cols = pl.ds(pl.multiple_of((6 * head + 3 * core + h) * HD, HD), HD)
                move(src.at[:, cols], dst.at[h, y], ss.at[h], rs.at[h], dp_of(to, core), here)

    for h in UPFRONT[0]:
        send_heads(h)

    wait(meta, meta_rs)
    wait(kv_raw, kv_rs)

    def masks_of():
        return [[meta[y_, SLOTS + r : SLOTS + r + 1, :] > 0.5 for y_ in range(NY)] for r in range(3)]

    def place(read, write, rounds):
        masks = masks_of()

        def rows(i, carry):
            at = pl.ds(pl.multiple_of(i * 16, 16), 16)
            tiles = exchange([read(y_, at) for y_ in range(NY)], masks, rounds)
            for y_ in range(NY):
                write(y_, at, tiles[y_].astype(BF16))
            return carry

        lax.fori_loop(0, TILE // 16, rows, 0)

    def write_kv(y_, at, value):
        kv[c, y_, 0, at, :] = value

    place(lambda y_, at: kv_raw[y_, at, :].astype(F32), write_kv, (0, 1, 2))

    halves = [pl.ds(half * HALF, HALF) for half in range(2)]
    for t in range(SLOTS):
        for half in range(2):
            tiles = halves[half]
            if t > 0:

                @pl.when(z >= t)
                def _():
                    wait(kv.at[0, tiles, t], kz_rs.at[t - 1, half])

            @pl.when(z >= t)
            def _():
                pltpu.make_async_remote_copy(
                    kv.at[c, tiles, t], kv.at[c, tiles, t], kc_ss.at[t, half], kc_rs.at[t, half],
                    device_id=(mate, z), device_id_type=MESH,
                ).start()

            if t < SLOTS - 1:

                @pl.when((z >= t) & (z < NZ - 1))
                def _():
                    pltpu.make_async_remote_copy(
                        kv.at[c, tiles, t], kv.at[c, tiles, t + 1], kz_ss.at[t, half], kz_rs.at[t, half],
                        device_id=(dp, z + 1), device_id_type=MESH,
                    ).start()

        if t in (0, 1):
            for h in UPFRONT[t + 1]:
                send_heads(h)

    for t in range(SLOTS):
        for half in range(2):

            @pl.when(z >= t)
            def _():
                wait(kv.at[0, halves[half], t], kc_rs.at[t, half])

    def attend(heads, first, last):
        n = len(heads)
        lanes = n * TILE
        h0, h1 = heads[0], heads[-1] + 1
        nt = (((1,), (1,)), ((), ()))
        row = lax.broadcasted_iota(jnp.int32, (TILE, lanes), 0)
        col = lax.rem(lax.broadcasted_iota(jnp.int32, (TILE, lanes), 1), TILE)

        def group(i, carry):
            step = (i + 1) // 2
            y_ = lax.rem(y + 2 * NY + (HALF - step) * (2 * lax.rem(i, 2) - 1), NY)
            keys = kv[0, y_].reshape(SLOTS * TILE, HD)
            values = kv[1, y_].reshape(SLOTS * TILE, HD)
            if first:
                kv_t[0, y_] = keys.T
                kv_t[1, y_] = values.T
            query = q_bal[h0:h1, y_].reshape(lanes, HD)
            grad = g_in[h0:h1, y_].reshape(lanes, HD)
            scores = lax.dot_general(keys, query, nt, preferred_element_type=F32)
            dprobs = lax.dot_general(values, grad, nt, preferred_element_type=F32)
            parts = [scores[t * TILE : (t + 1) * TILE] for t in range(SLOTS)]
            parts[0] = jnp.where(row <= col, parts[0], FAR)
            bias = [jnp.concatenate([meta[y_, t : t + 1, :]] * n, axis=1) for t in range(SLOTS)]
            peaks = [jnp.max(parts[t], axis=0, keepdims=True) + bias[t] for t in range(SLOTS)]
            peak = functools.reduce(jnp.maximum, peaks)
            parts = [jnp.exp2((parts[t] - (peak - bias[t])) * (SCALE * LOG2E)) for t in range(SLOTS)]
            total = functools.reduce(jnp.add, [jnp.sum(part, axis=0, keepdims=True) for part in parts])
            inverse = 1.0 / total
            probs = jnp.concatenate([part * inverse for part in parts], axis=0)
            weights = probs.astype(BF16)
            delta = jnp.sum(probs * dprobs, axis=0, keepdims=True)
            dscores = (probs * (dprobs - delta)).astype(BF16)
            out_t = jnp.dot(kv_t[1, y_], weights, preferred_element_type=F32)
            o_buf[h0:h1, y_] = out_t.T.astype(BF16).reshape(n, TILE, HD)
            dq_t = jnp.dot(kv_t[0, y_], dscores, preferred_element_type=F32) * SCALE
            dq_bal[h0:h1, y_] = dq_t.T.astype(BF16).reshape(n, TILE, HD)
            dk = jnp.dot(dscores, query, preferred_element_type=F32).reshape(SLOTS, TILE, HD)
            dv = jnp.dot(weights, grad, preferred_element_type=F32).reshape(SLOTS, TILE, HD)
            if first:
                acc[0, i] = dk
                acc[1, i] = dv
            else:
                acc[0, i] += dk
                acc[1, i] += dv
            here = (y_ == y) & (own == c)
            for h in heads:
                cols = pl.ds(pl.multiple_of((6 * kv_head + 3 * c + h) * HD, HD), HD)
                move(o_buf.at[h, y_], out_ref.at[:, cols], o_ss.at[h], o_rs, dp_of(y_, own), here)
            if last:
                pair_out[i] = acc[other, i].astype(BF16)
                part = i // PART
                pltpu.make_async_remote_copy(
                    pair_out.at[i], pair_in.at[i], pc_ss.at[part], pc_rs.at[part],
                    device_id=(mate, z), device_id_type=MESH,
                ).start()
            return carry

        for h in heads:
            wait(q_raw.at[h], q_rs.at[h])

            def write_q(y_, at, value, h=h):
                q_bal[h, y_, at, :] = value

            place(lambda y_, at, h=h: q_raw[h, y_, at, :].astype(F32), write_q, (0, 1, 2))
        for h in heads:
            wait(g_in.at[h], g_rs.at[h])
        if not last:
            lax.fori_loop(0, NY, group, 0, unroll=2)
            return

        def some(part, carry):
            for i in range(PART):
                group(part * PART + i, carry)

            @pl.when(part > 0)
            def _():
                chain_step(SLOTS - 1, part - 1)

            return carry

        lax.fori_loop(0, PARTS, some, 0)

    def send_dq(heads):
        for h in heads:

            def write_dq(y_, at, value, h=h):
                dq_buf[h, y_, at, :] = value

            place(lambda y_, at, h=h: dq_bal[h, y_, at, :].astype(F32), write_dq, (2, 1, 0))
            cols = pl.ds(pl.multiple_of((6 * kv_head + 3 * c + h) * HD, HD), HD)
            for i in ORDER:
                to = lax.rem(y + i, NY)
                here = (to == y) & (own == c)
                move(dq_buf.at[h, to], dq_ref.at[:, cols], dq_ss.at[h], dq_rs, dp_of(to, own), here)

    attend((0, 1), True, False)
    send_dq((0, 1))

    def chain_step(t, part):
        tiles = pl.ds(part * PART, PART)
        if t == SLOTS - 1:
            wait(pair_in.at[tiles], pc_rs.at[part])

        @pl.when(z >= t)
        def _():
            if t < SLOTS - 1:

                @pl.when(z < NZ - 1)
                def _():
                    wait(chain_in.at[t, tiles], cz_rs.at[t, part])

            total = acc[c, tiles, t] + pair_in[tiles, t].astype(F32)
            if t < SLOTS - 1:
                total = total + chain_in[t, tiles].astype(F32)
            chain_out[t - 1, tiles] = total.astype(BF16)
            pltpu.make_async_remote_copy(
                chain_out.at[t - 1, tiles], chain_in.at[t - 1, tiles],
                cz_ss.at[t - 1, part], cz_rs.at[t - 1, part],
                device_id=(dp, z - 1), device_id_type=MESH,
            ).start()

    attend((2,), False, True)
    chain_step(SLOTS - 1, PARTS - 1)
    send_dq((2,))
    for t in reversed(range(1, SLOTS - 1)):

        def step(part, carry, t=t):
            chain_step(t, part)
            return carry

        lax.fori_loop(0, PARTS, step, 0)


    @pl.when(z < NZ - 1)
    def _():
        for part in range(PARTS):
            wait(chain_in.at[0, part * PART : (part + 1) * PART], cz_rs.at[0, part])

    factor = jnp.where(c == 0, SCALE, 1.0).astype(F32)

    def read_total(y_, at):
        d = lax.rem(y_ - y + NY, NY)
        i = (d // HALF) * (2 * (d - HALF)) + (1 - d // HALF) * (NY - 1 - 2 * d)
        total = acc[c, i, 0, at, :] + pair_in[i, 0, at, :].astype(F32) + chain_in[0, i, at, :].astype(F32)
        return total * factor

    def write_total(y_, at, value):
        fin[y_, at, :] = value

    place(read_total, write_total, (2, 1, 0))
    cols = pl.ds(pl.multiple_of(kv_head * HD, HD), HD)
    for i in ORDER:
        to = lax.rem(y + i, NY)
        here = (to == y) & (own == c)

        @pl.when(c == 0)
        def _():
            move(fin.at[to], dk_ref.at[:, cols], f_ss, f_rs.at[0], dp_of(to, own), here)

        @pl.when(c == 1)
        def _():
            move(fin.at[to], dv_ref.at[:, cols], f_ss, f_rs.at[1], dp_of(to, own), here)

    wait(out_ref, o_rs)
    wait(dq_ref, dq_rs)
    wait(dk_ref, f_rs.at[0])
    wait(dv_ref, f_rs.at[1])
    wait_sent(meta, meta_ss)
    wait_sent(kv_raw, kv_ss)
    wait_sent(fin, f_ss)
    for h in range(NH):
        wait_sent(q_raw.at[h], q_ss.at[h])
        wait_sent(g_in.at[h], g_ss.at[h])
        wait_sent(o_buf.at[h], o_ss.at[h])
        wait_sent(dq_buf.at[h], dq_ss.at[h])
    for half in range(2):
        tiles = halves[half]
        for t in range(SLOTS):

            @pl.when(z >= t)
            def _():
                wait(kv.at[0, tiles, t], kc_ss.at[t, half])

        for t in range(SLOTS - 1):

            @pl.when((z >= t) & (z < NZ - 1))
            def _():
                wait(kv.at[0, tiles, t], kz_ss.at[t, half])

    for part in range(PARTS):
        tiles = pl.ds(part * PART, PART)
        wait(pair_out.at[tiles], pc_ss.at[part])
        for t in range(SLOTS - 1):

            @pl.when(z >= t + 1)
            def _():
                wait(chain_out.at[t, tiles], cz_ss.at[t, part])


def hand_over(*refs):
    copies = [pltpu.make_async_copy(refs[i], refs[4 + i], refs[8].at[i]) for i in range(4)]
    for copy in copies:
        copy.start()
    for copy in copies:
        copy.wait()


def on_device(q_in, k_in, v_in, dout, swap_plan, doc_ids):
    tile = (TILE, HD)
    dma = pltpu.SemaphoreType.DMA
    hbm, smem = pl.BlockSpec(memory_space=pl.ANY), pl.BlockSpec(memory_space=pltpu.SMEM)
    results = pl.pallas_call(
        kernel,
        out_shape=[pltpu.VMEM(a.shape, BF16) for a in (dout, q_in, k_in, v_in)],
        in_specs=[smem, smem, hbm, hbm, hbm, hbm],
        out_specs=[hbm] * 4,
        scratch_shapes=[
            pltpu.VMEM((8, HD), F32),
            pltpu.VMEM((NY, 8, HD), F32),
            pltpu.VMEM((NY, *tile), BF16),
            pltpu.VMEM((2, NY, SLOTS, *tile), BF16),
            pltpu.VMEM((2, NY, HD, SLOTS * TILE), BF16),
            pltpu.VMEM((NH, NY, *tile), BF16),
            pltpu.VMEM((NH, NY, *tile), BF16),
            pltpu.VMEM((NH, NY, *tile), BF16),
            pltpu.VMEM((NH, NY, *tile), BF16),
            pltpu.VMEM((NH, NY, *tile), BF16),
            pltpu.VMEM((NH, NY, *tile), BF16),
            pltpu.VMEM((2, NY, SLOTS, *tile), F32),
            pltpu.VMEM((NY, SLOTS, *tile), BF16),
            pltpu.VMEM((NY, SLOTS, *tile), BF16),
            pltpu.VMEM((SLOTS - 1, NY, *tile), BF16),
            pltpu.VMEM((SLOTS - 1, NY, *tile), BF16),
            pltpu.VMEM((NY, *tile), BF16),
            dma, dma, dma, dma,
            dma((NH,)), dma((NH,)), dma((NH,)), dma((NH,)),
            dma((SLOTS - 1, 2)), dma((SLOTS - 1, 2)), dma((SLOTS, 2)), dma((SLOTS, 2)),
            dma((NH,)), dma, dma((NH,)), dma,
            dma((PARTS,)), dma((PARTS,)), dma((SLOTS - 1, PARTS)), dma((SLOTS - 1, PARTS)),
            dma, dma((2,)),
        ],
        compiler_params=pltpu.CompilerParams(
            collective_id=0, has_side_effects=True, vmem_limit_bytes=62 << 20
        ),
    )(swap_plan.reshape(1, 3), doc_ids, q_in, k_in, v_in, dout)
    return pl.pallas_call(
        hand_over,
        out_shape=[jax.ShapeDtypeStruct(a.shape, BF16) for a in results],
        in_specs=[pl.BlockSpec(memory_space=pltpu.VMEM)] * 4,
        out_specs=[hbm] * 4,
        scratch_shapes=[dma((4,))],
        compiler_params=pltpu.CompilerParams(vmem_limit_bytes=1 << 20),
    )(*[pltpu.with_memory_space_constraint(a, pltpu.VMEM) for a in results])


def solution(mesh):
    rows = P(("dp", "head"), None)
    return jax.shard_map(
        on_device,
        mesh=mesh,
        in_specs=(rows, rows, rows, rows, P(None, ("dp", "head")), P("dp", None)),
        out_specs=(rows, rows, rows, rows),
        check_vma=False,
    )
```

```python
import functools

import jax
import jax.numpy as jnp
from jax import lax
from jax.experimental import pallas as pl
from jax.experimental.pallas import tpu as pltpu
from jax.sharding import PartitionSpec as P

HD = 128
TILE = 128
NY = 8
NX = 4
NZ = 8
NH = 3
HALF = NY // 2
PARTS = 4
PART = NY // PARTS
CUT = TILE // 2
SLOTS = 5
SCALE = HD**-0.5
LOG2E = 1.4426950408889634
FAR = -1e30
MESH = pl.DeviceIdType.MESH
UPFRONT = ((0, 1, 2), (), ())
F32 = jnp.float32
BF16 = jnp.bfloat16


ORDER = (4, 3, 5, 2, 6, 1, 7, 0)


def exchange(tiles, masks, rounds):
    tiles = list(tiles)
    for r in rounds:
        stride = 4 >> r
        tiles = [jnp.where(masks[r][y], tiles[y ^ stride], tiles[y]) for y in range(NY)]
    return tiles


def kernel(
    swap_ref, docs_ref, q_ref, k_ref, v_ref, g_ref,
    out_ref, dq_ref, dk_ref, dv_ref,
    meta_src, meta, kv_raw, kv, kv_t, q_raw, q_bal, g_in,
    o_buf, dq_bal, dq_buf, acc, pair_out, pair_in, chain_out, chain_in, fin,
    meta_ss, meta_rs, kv_ss, kv_rs, q_ss, q_rs, g_ss, g_rs,
    kz_ss, kz_rs, kc_ss, kc_rs, o_ss, o_rs, dq_ss, dq_rs,
    pc_ss, pc_rs, cz_ss, cz_rs, f_ss, f_rs,
):
    dp = lax.axis_index("dp")
    z = lax.axis_index("head")
    y, x, c = dp // (2 * NX), (dp // 2) % NX, dp % 2
    own, other = y % 2, 1 - c
    kv_head = y // 2
    mate = dp + 1 - 2 * c

    def dp_of(yy, cc):
        return (yy * NX + x) * 2 + cc

    def move(src, dst, send_sem, recv_sem, target, here):
        @pl.when(jnp.logical_not(here))
        def _():
            pltpu.make_async_remote_copy(
                src, dst, send_sem, recv_sem, device_id=(target, z), device_id_type=MESH
            ).start()

        @pl.when(here)
        def _():
            pltpu.make_async_copy(src, dst, recv_sem).start()

    def wait(ref, sem):
        pltpu.make_async_copy(ref, ref, sem).wait()

    def wait_sent(ref, sem):
        @pl.when(own == c)
        def _():
            wait(ref.at[0 : NY - 1], sem)

        @pl.when(own != c)
        def _():
            wait(ref, sem)

    barrier = pltpu.get_barrier_semaphore()
    me = y * 2 + c
    for step in range(1, 16):
        peer = lax.rem(me + step, 16)
        pl.semaphore_signal(barrier, inc=1, device_id=(dp_of(peer // 2, peer % 2), z), device_id_type=MESH)

    @pl.when(z < NZ - 1)
    def _():
        pl.semaphore_signal(barrier, inc=1, device_id=(dp, z + 1), device_id_type=MESH)

    @pl.when(z > 0)
    def _():
        pl.semaphore_signal(barrier, inc=1, device_id=(dp, z - 1), device_id_type=MESH)

    mine = docs_ref[0, z]
    meta_src[0:1, :] = jnp.zeros((1, HD), F32)
    for t in range(1, SLOTS):
        same = (docs_ref[0, jnp.maximum(z - t, 0)] == mine) & (z >= t)
        meta_src[t : t + 1, :] = jnp.full((1, HD), jnp.where(same, 0.0, FAR), F32)
    for r in range(3):
        meta_src[SLOTS + r : SLOTS + r + 1, :] = jnp.full((1, HD), swap_ref[0, r].astype(F32), F32)

    for t in range(1, SLOTS):

        @pl.when(z < t)
        def _():
            kv[:, :, t] = jnp.zeros((2, NY, TILE, HD), BF16)

    @pl.when(z == NZ - 1)
    def _():
        chain_in[...] = jnp.zeros_like(chain_in)

    @pl.when((z > 0) & (z < NZ - 1))
    def _():
        pl.semaphore_wait(barrier, 17)

    @pl.when((z == 0) | (z == NZ - 1))
    def _():
        pl.semaphore_wait(barrier, 16)

    dests = []
    for i in (2, 1, 3, 0):
        for j in range(2):
            head, core = lax.rem(kv_head + i, 4), lax.rem(c + j, 2)
            to = 2 * head + c
            dests.append((head, core, to, (to == y) & (core == c)))
    for head, core, to, here in dests:
        move(meta_src, meta.at[y], meta_ss, meta_rs, dp_of(to, core), here)
    for head, core, to, here in dests:
        cols = pl.ds(pl.multiple_of(head * HD, HD), HD)

        @pl.when(core == 0)
        def _():
            move(k_ref.at[:, cols], kv_raw.at[y], kv_ss, kv_rs, dp_of(to, core), here)

        @pl.when(core == 1)
        def _():
            move(v_ref.at[:, cols], kv_raw.at[y], kv_ss, kv_rs, dp_of(to, core), here)

    def send_heads(h):
        for src, dst, ss, rs in ((q_ref, q_raw, q_ss, q_rs), (g_ref, g_in, g_ss, g_rs)):
            for head, core, to, here in dests:
                cols = pl.ds(pl.multiple_of((6 * head + 3 * core + h) * HD, HD), HD)
                move(src.at[:, cols], dst.at[h, y], ss.at[h], rs.at[h], dp_of(to, core), here)

    for h in UPFRONT[0]:
        send_heads(h)

    wait(meta, meta_rs)
    wait(kv_raw, kv_rs)

    def masks_of():
        return [[meta[y_, SLOTS + r : SLOTS + r + 1, :] > 0.5 for y_ in range(NY)] for r in range(3)]

    def place(read, write, rounds, start=0, count=TILE):
        masks = masks_of()

        def rows(i, carry):
            at = pl.ds(pl.multiple_of(start + i * 16, 16), 16)
            tiles = exchange([read(y_, at) for y_ in range(NY)], masks, rounds)
            for y_ in range(NY):
                write(y_, at, tiles[y_].astype(BF16))
            return carry

        lax.fori_loop(0, count // 16, rows, 0)

    def write_kv(y_, at, value):
        kv[c, y_, 0, at, :] = value

    place(lambda y_, at: kv_raw[y_, at, :].astype(F32), write_kv, (0, 1, 2))

    halves = [pl.ds(half * HALF, HALF) for half in range(2)]
    for t in range(SLOTS):
        for half in range(2):
            tiles = halves[half]
            if t > 0:

                @pl.when(z >= t)
                def _():
                    wait(kv.at[0, tiles, t], kz_rs.at[t - 1, half])

            @pl.when(z >= t)
            def _():
                pltpu.make_async_remote_copy(
                    kv.at[c, tiles, t], kv.at[c, tiles, t], kc_ss.at[t, half], kc_rs.at[t, half],
                    device_id=(mate, z), device_id_type=MESH,
                ).start()

            if t < SLOTS - 1:

                @pl.when((z >= t) & (z < NZ - 1))
                def _():
                    pltpu.make_async_remote_copy(
                        kv.at[c, tiles, t], kv.at[c, tiles, t + 1], kz_ss.at[t, half], kz_rs.at[t, half],
                        device_id=(dp, z + 1), device_id_type=MESH,
                    ).start()

        if t in (0, 1):
            for h in UPFRONT[t + 1]:
                send_heads(h)

    for t in range(SLOTS):
        for half in range(2):

            @pl.when(z >= t)
            def _():
                wait(kv.at[0, halves[half], t], kc_rs.at[t, half])

    def attend(heads, first, last):
        n = len(heads)
        lanes = n * TILE
        h0, h1 = heads[0], heads[-1] + 1
        nt = (((1,), (1,)), ((), ()))
        row = lax.broadcasted_iota(jnp.int32, (TILE, lanes), 0)
        col = lax.rem(lax.broadcasted_iota(jnp.int32, (TILE, lanes), 1), TILE)

        def group(i, carry):
            step = (i + 1) // 2
            y_ = lax.rem(y + 2 * NY + (HALF - step) * (2 * lax.rem(i, 2) - 1), NY)
            keys = kv[0, y_].reshape(SLOTS * TILE, HD)
            values = kv[1, y_].reshape(SLOTS * TILE, HD)
            if first:
                kv_t[0, y_] = keys.T
                kv_t[1, y_] = values.T
            query = q_bal[h0:h1, y_].reshape(lanes, HD)
            grad = g_in[h0:h1, y_].reshape(lanes, HD)
            scores = lax.dot_general(keys, query, nt, preferred_element_type=F32)
            dprobs = lax.dot_general(values, grad, nt, preferred_element_type=F32)
            parts = [scores[t * TILE : (t + 1) * TILE] for t in range(SLOTS)]
            parts[0] = jnp.where(row <= col, parts[0], FAR)
            bias = [jnp.concatenate([meta[y_, t : t + 1, :]] * n, axis=1) for t in range(SLOTS)]
            peaks = [jnp.max(parts[t], axis=0, keepdims=True) + bias[t] for t in range(SLOTS)]
            peak = functools.reduce(jnp.maximum, peaks)
            parts = [jnp.exp2((parts[t] - (peak - bias[t])) * (SCALE * LOG2E)) for t in range(SLOTS)]
            total = functools.reduce(jnp.add, [jnp.sum(part, axis=0, keepdims=True) for part in parts])
            inverse = 1.0 / total
            probs = jnp.concatenate([part * inverse for part in parts], axis=0)
            weights = probs.astype(BF16)
            delta = jnp.sum(probs * dprobs, axis=0, keepdims=True)
            dscores = (probs * (dprobs - delta)).astype(BF16)
            out_t = jnp.dot(kv_t[1, y_], weights, preferred_element_type=F32)
            o_buf[h0:h1, y_] = out_t.T.astype(BF16).reshape(n, TILE, HD)
            dq_t = jnp.dot(kv_t[0, y_], dscores, preferred_element_type=F32) * SCALE
            dq_bal[h0:h1, y_] = dq_t.T.astype(BF16).reshape(n, TILE, HD)
            dk = jnp.dot(dscores, query, preferred_element_type=F32).reshape(SLOTS, TILE, HD)
            dv = jnp.dot(weights, grad, preferred_element_type=F32).reshape(SLOTS, TILE, HD)
            if first:
                acc[0, i] = dk
                acc[1, i] = dv
            else:
                acc[0, i] += dk
                acc[1, i] += dv
            here = (y_ == y) & (own == c)
            for h in heads:
                cols = pl.ds(pl.multiple_of((6 * kv_head + 3 * c + h) * HD, HD), HD)
                move(o_buf.at[h, y_], out_ref.at[:, cols], o_ss.at[h], o_rs, dp_of(y_, own), here)
            if last:
                pair_out[i] = acc[other, i].astype(BF16)
                part = i // PART
                pltpu.make_async_remote_copy(
                    pair_out.at[i], pair_in.at[i], pc_ss.at[part], pc_rs.at[part],
                    device_id=(mate, z), device_id_type=MESH,
                ).start()
            return carry

        for h in heads:
            wait(q_raw.at[h], q_rs.at[h])

            def write_q(y_, at, value, h=h):
                q_bal[h, y_, at, :] = value

            place(lambda y_, at, h=h: q_raw[h, y_, at, :].astype(F32), write_q, (0, 1, 2))
        for h in heads:
            wait(g_in.at[h], g_rs.at[h])
        if not last:
            lax.fori_loop(0, NY, group, 0, unroll=2)
            return

        def some(part, carry):
            for i in range(PART):
                group(part * PART + i, carry)

            @pl.when(part > 0)
            def _():
                chain_begin(part - 1)

            return carry

        lax.fori_loop(0, PARTS, some, 0)

    def send_dq(heads):
        for h in heads:

            def write_dq(y_, at, value, h=h):
                dq_buf[h, y_, at, :] = value

            place(lambda y_, at, h=h: dq_bal[h, y_, at, :].astype(F32), write_dq, (2, 1, 0))
            cols = pl.ds(pl.multiple_of((6 * kv_head + 3 * c + h) * HD, HD), HD)
            for i in ORDER:
                to = lax.rem(y + i, NY)
                here = (to == y) & (own == c)
                move(dq_buf.at[h, to], dq_ref.at[:, cols], dq_ss.at[h], dq_rs, dp_of(to, own), here)

    attend((0, 1), True, False)
    send_dq((0, 1))

    def chain_step(t, part, cut):
        tiles, rows = pl.ds(part * PART, PART), pl.ds(cut * CUT, CUT)

        @pl.when(z >= t)
        def _():
            if t < SLOTS - 1:

                @pl.when(z < NZ - 1)
                def _():
                    wait(chain_in.at[t, tiles, rows], cz_rs.at[t, part, cut])

            total = acc[c, tiles, t, rows] + pair_in[tiles, t, rows].astype(F32)
            if t < SLOTS - 1:
                total = total + chain_in[t, tiles, rows].astype(F32)
            chain_out[t - 1, tiles, rows] = total.astype(BF16)
            pltpu.make_async_remote_copy(
                chain_out.at[t - 1, tiles, rows], chain_in.at[t - 1, tiles, rows],
                cz_ss.at[t - 1, part, cut], cz_rs.at[t - 1, part, cut],
                device_id=(dp, z - 1), device_id_type=MESH,
            ).start()

    def chain_begin(part):
        wait(pair_in.at[pl.ds(part * PART, PART)], pc_rs.at[part])
        for cut in range(2):
            chain_step(SLOTS - 1, part, cut)

    attend((2,), False, True)
    chain_begin(PARTS - 1)
    send_dq((2,))
    for t in reversed(range(1, SLOTS - 1)):

        for cut in range(2):

            def step(part, carry, t=t, cut=cut):
                chain_step(t, part, cut)
                return carry

            lax.fori_loop(0, PARTS, step, 0)


    factor = jnp.where(c == 0, SCALE, 1.0).astype(F32)

    def read_total(y_, at):
        d = lax.rem(y_ - y + NY, NY)
        i = (d // HALF) * (2 * (d - HALF)) + (1 - d // HALF) * (NY - 1 - 2 * d)
        total = acc[c, i, 0, at, :] + pair_in[i, 0, at, :].astype(F32) + chain_in[0, i, at, :].astype(F32)
        return total * factor

    def write_total(y_, at, value):
        fin[y_, at, :] = value

    cols = pl.ds(pl.multiple_of(kv_head * HD, HD), HD)
    for cut in range(2):
        rows = pl.ds(cut * CUT, CUT)

        @pl.when(z < NZ - 1)
        def _():
            for part in range(PARTS):
                wait(chain_in.at[0, part * PART : (part + 1) * PART, rows], cz_rs.at[0, part, cut])

        place(read_total, write_total, (2, 1, 0), cut * CUT, CUT)
        for i in ORDER:
            to = lax.rem(y + i, NY)
            here = (to == y) & (own == c)

            @pl.when(c == 0)
            def _():
                move(fin.at[to, rows], dk_ref.at[rows, cols], f_ss.at[cut], f_rs.at[0], dp_of(to, own), here)

            @pl.when(c == 1)
            def _():
                move(fin.at[to, rows], dv_ref.at[rows, cols], f_ss.at[cut], f_rs.at[1], dp_of(to, own), here)

    wait(out_ref, o_rs)
    wait(dq_ref, dq_rs)
    wait(dk_ref, f_rs.at[0])
    wait(dv_ref, f_rs.at[1])
    wait_sent(meta, meta_ss)
    wait_sent(kv_raw, kv_ss)
    for cut in range(2):
        wait_sent(fin.at[:, cut * CUT : (cut + 1) * CUT], f_ss.at[cut])
    for h in range(NH):
        wait_sent(q_raw.at[h], q_ss.at[h])
        wait_sent(g_in.at[h], g_ss.at[h])
        wait_sent(o_buf.at[h], o_ss.at[h])
        wait_sent(dq_buf.at[h], dq_ss.at[h])
    for half in range(2):
        tiles = halves[half]
        for t in range(SLOTS):

            @pl.when(z >= t)
            def _():
                wait(kv.at[0, tiles, t], kc_ss.at[t, half])

        for t in range(SLOTS - 1):

            @pl.when((z >= t) & (z < NZ - 1))
            def _():
                wait(kv.at[0, tiles, t], kz_ss.at[t, half])

    for part in range(PARTS):
        tiles = pl.ds(part * PART, PART)
        wait(pair_out.at[tiles], pc_ss.at[part])
        for t in range(SLOTS - 1):

            @pl.when(z >= t + 1)
            def _():
                for cut in range(2):
                    wait(chain_out.at[t, tiles, cut * CUT : (cut + 1) * CUT], cz_ss.at[t, part, cut])


def hand_over(*refs):
    copies = [pltpu.make_async_copy(refs[i], refs[4 + i], refs[8].at[i]) for i in range(4)]
    for copy in copies:
        copy.start()
    for copy in copies:
        copy.wait()


def on_device(q_in, k_in, v_in, dout, swap_plan, doc_ids):
    tile = (TILE, HD)
    dma = pltpu.SemaphoreType.DMA
    hbm, smem = pl.BlockSpec(memory_space=pl.ANY), pl.BlockSpec(memory_space=pltpu.SMEM)
    results = pl.pallas_call(
        kernel,
        out_shape=[pltpu.VMEM(a.shape, BF16) for a in (dout, q_in, k_in, v_in)],
        in_specs=[smem, smem, hbm, hbm, hbm, hbm],
        out_specs=[hbm] * 4,
        scratch_shapes=[
            pltpu.VMEM((8, HD), F32),
            pltpu.VMEM((NY, 8, HD), F32),
            pltpu.VMEM((NY, *tile), BF16),
            pltpu.VMEM((2, NY, SLOTS, *tile), BF16),
            pltpu.VMEM((2, NY, HD, SLOTS * TILE), BF16),
            pltpu.VMEM((NH, NY, *tile), BF16),
            pltpu.VMEM((NH, NY, *tile), BF16),
            pltpu.VMEM((NH, NY, *tile), BF16),
            pltpu.VMEM((NH, NY, *tile), BF16),
            pltpu.VMEM((NH, NY, *tile), BF16),
            pltpu.VMEM((NH, NY, *tile), BF16),
            pltpu.VMEM((2, NY, SLOTS, *tile), F32),
            pltpu.VMEM((NY, SLOTS, *tile), BF16),
            pltpu.VMEM((NY, SLOTS, *tile), BF16),
            pltpu.VMEM((SLOTS - 1, NY, *tile), BF16),
            pltpu.VMEM((SLOTS - 1, NY, *tile), BF16),
            pltpu.VMEM((NY, *tile), BF16),
            dma, dma, dma, dma,
            dma((NH,)), dma((NH,)), dma((NH,)), dma((NH,)),
            dma((SLOTS - 1, 2)), dma((SLOTS - 1, 2)), dma((SLOTS, 2)), dma((SLOTS, 2)),
            dma((NH,)), dma, dma((NH,)), dma,
            dma((PARTS,)), dma((PARTS,)), dma((SLOTS - 1, PARTS, 2)), dma((SLOTS - 1, PARTS, 2)),
            dma((2,)), dma((2,)),
        ],
        compiler_params=pltpu.CompilerParams(
            collective_id=0, has_side_effects=True, vmem_limit_bytes=62 << 20
        ),
    )(swap_plan.reshape(1, 3), doc_ids, q_in, k_in, v_in, dout)
    return pl.pallas_call(
        hand_over,
        out_shape=[jax.ShapeDtypeStruct(a.shape, BF16) for a in results],
        in_specs=[pl.BlockSpec(memory_space=pltpu.VMEM)] * 4,
        out_specs=[hbm] * 4,
        scratch_shapes=[dma((4,))],
        compiler_params=pltpu.CompilerParams(vmem_limit_bytes=1 << 20),
    )(*[pltpu.with_memory_space_constraint(a, pltpu.VMEM) for a in results])


def solution(mesh):
    rows = P(("dp", "head"), None)
    return jax.shard_map(
        on_device,
        mesh=mesh,
        in_specs=(rows, rows, rows, rows, P(None, ("dp", "head")), P("dp", None)),
        out_specs=(rows, rows, rows, rows),
        check_vma=False,
    )
```

```python
import functools

import jax
import jax.numpy as jnp
from jax import lax
from jax.experimental import pallas as pl
from jax.experimental.pallas import tpu as pltpu
from jax.sharding import PartitionSpec as P

HD = 128
TILE = 128
NY = 8
NX = 4
NZ = 8
NH = 3
HALF = NY // 2
PARTS = 4
PART = NY // PARTS
CUT = TILE // 2
SLOTS = 5
SCALE = HD**-0.5
LOG2E = 1.4426950408889634
FAR = -1e30
MESH = pl.DeviceIdType.MESH
F32 = jnp.float32
BF16 = jnp.bfloat16


ORDER = (4, 3, 5, 2, 6, 1, 7, 0)


def exchange(tiles, masks, rounds):
    tiles = list(tiles)
    for r in rounds:
        stride = 4 >> r
        tiles = [jnp.where(masks[r][y], tiles[y ^ stride], tiles[y]) for y in range(NY)]
    return tiles


def kernel(
    swap_ref, docs_ref, q_ref, k_ref, v_ref, g_ref,
    out_ref, dq_ref, dk_ref, dv_ref,
    meta_src, meta, kv_raw, kv, kv_t, q_raw, q_bal, g_in,
    o_buf, dq_bal, dq_buf, acc, pair_out, pair_in, chain_out, chain_in, fin,
    meta_ss, meta_rs, kv_ss, kv_rs, q_ss, q_rs, g_ss, g_rs,
    kz_ss, kz_rs, kc_ss, kc_rs, o_ss, o_rs, dq_ss, dq_rs,
    pc_ss, pc_rs, cz_ss, cz_rs, f_ss, f_rs,
):
    dp = lax.axis_index("dp")
    z = lax.axis_index("head")
    y, x, c = dp // (2 * NX), (dp // 2) % NX, dp % 2
    own, other = y % 2, 1 - c
    kv_head = y // 2
    mate = dp + 1 - 2 * c

    def dp_of(yy, cc):
        return (yy * NX + x) * 2 + cc

    def move(src, dst, send_sem, recv_sem, target, here):
        @pl.when(jnp.logical_not(here))
        def _():
            pltpu.make_async_remote_copy(
                src, dst, send_sem, recv_sem, device_id=(target, z), device_id_type=MESH
            ).start()

        @pl.when(here)
        def _():
            pltpu.make_async_copy(src, dst, recv_sem).start()

    def wait(ref, sem):
        pltpu.make_async_copy(ref, ref, sem).wait()

    def wait_sent(ref, sem):
        @pl.when(own == c)
        def _():
            wait(ref.at[0 : NY - 1], sem)

        @pl.when(own != c)
        def _():
            wait(ref, sem)

    barrier = pltpu.get_barrier_semaphore()
    me = y * 2 + c
    for step in range(1, 16):
        peer = lax.rem(me + step, 16)
        pl.semaphore_signal(barrier, inc=1, device_id=(dp_of(peer // 2, peer % 2), z), device_id_type=MESH)

    @pl.when(z < NZ - 1)
    def _():
        pl.semaphore_signal(barrier, inc=1, device_id=(dp, z + 1), device_id_type=MESH)

    @pl.when(z > 0)
    def _():
        pl.semaphore_signal(barrier, inc=1, device_id=(dp, z - 1), device_id_type=MESH)

    mine = docs_ref[0, z]
    meta_src[0:1, :] = jnp.zeros((1, HD), F32)
    for t in range(1, SLOTS):
        same = (docs_ref[0, jnp.maximum(z - t, 0)] == mine) & (z >= t)
        meta_src[t : t + 1, :] = jnp.full((1, HD), jnp.where(same, 0.0, FAR), F32)
    for r in range(3):
        meta_src[SLOTS + r : SLOTS + r + 1, :] = jnp.full((1, HD), swap_ref[0, r].astype(F32), F32)

    for t in range(1, SLOTS):

        @pl.when(z < t)
        def _():
            kv[:, :, t] = jnp.zeros((2, NY, TILE, HD), BF16)

    @pl.when(z == NZ - 1)
    def _():
        chain_in[...] = jnp.zeros_like(chain_in)

    @pl.when((z > 0) & (z < NZ - 1))
    def _():
        pl.semaphore_wait(barrier, 17)

    @pl.when((z == 0) | (z == NZ - 1))
    def _():
        pl.semaphore_wait(barrier, 16)

    dests = []
    for i in (2, 1, 3, 0):
        for j in range(2):
            head, core = lax.rem(kv_head + i, 4), lax.rem(c + j, 2)
            to = 2 * head + c
            dests.append((head, core, to, (to == y) & (core == c)))
    for head, core, to, here in dests:
        move(meta_src, meta.at[y], meta_ss, meta_rs, dp_of(to, core), here)
    for head, core, to, here in dests:
        cols = pl.ds(pl.multiple_of(head * HD, HD), HD)

        @pl.when(core == 0)
        def _():
            move(k_ref.at[:, cols], kv_raw.at[y], kv_ss, kv_rs, dp_of(to, core), here)

        @pl.when(core == 1)
        def _():
            move(v_ref.at[:, cols], kv_raw.at[y], kv_ss, kv_rs, dp_of(to, core), here)

    def send_heads(h):
        for src, dst, ss, rs in ((q_ref, q_raw, q_ss, q_rs), (g_ref, g_in, g_ss, g_rs)):
            for head, core, to, here in dests:
                cols = pl.ds(pl.multiple_of((6 * head + 3 * core + h) * HD, HD), HD)
                move(src.at[:, cols], dst.at[h, y], ss.at[h], rs.at[h], dp_of(to, core), here)

    for h in range(NH):
        send_heads(h)

    wait(meta, meta_rs)
    wait(kv_raw, kv_rs)

    def masks_of():
        return [[meta[y_, SLOTS + r : SLOTS + r + 1, :] > 0.5 for y_ in range(NY)] for r in range(3)]

    def place(read, write, rounds, start=0, count=TILE):
        masks = masks_of()

        def rows(i, carry):
            at = pl.ds(pl.multiple_of(start + i * 16, 16), 16)
            tiles = exchange([read(y_, at) for y_ in range(NY)], masks, rounds)
            for y_ in range(NY):
                write(y_, at, tiles[y_].astype(BF16))
            return carry

        lax.fori_loop(0, count // 16, rows, 0)

    def turn(y_):
        d = lax.rem(y_ - y + NY, NY)
        return (d // HALF) * (2 * (d - HALF)) + (1 - d // HALF) * (NY - 1 - 2 * d)

    def write_kv(y_, at, value):
        kv[c, turn(y_), 0, at, :] = value

    place(lambda y_, at: kv_raw[y_, at, :].astype(F32), write_kv, (0, 1, 2))

    def key_step(t, part):
        tiles = pl.ds(part * PART, PART)

        @pl.when(z >= t)
        def _():
            if t > 0:
                wait(kv.at[0, tiles, t], kz_rs.at[t - 1, part])
            pltpu.make_async_remote_copy(
                kv.at[c, tiles, t], kv.at[c, tiles, t], kc_ss.at[t, part], kc_rs.at[t, part],
                device_id=(mate, z), device_id_type=MESH,
            ).start()

        if t < SLOTS - 1:

            @pl.when((z >= t) & (z < NZ - 1))
            def _():
                pltpu.make_async_remote_copy(
                    kv.at[c, tiles, t], kv.at[c, tiles, t + 1], kz_ss.at[t, part], kz_rs.at[t, part],
                    device_id=(dp, z + 1), device_id_type=MESH,
                ).start()

    for t in range(SLOTS - 1):
        for part in range(PARTS):
            key_step(t, part)

    def attend(heads, first, last):
        n = len(heads)
        lanes = n * TILE
        h0, h1 = heads[0], heads[-1] + 1
        nt = (((1,), (1,)), ((), ()))
        row = lax.broadcasted_iota(jnp.int32, (TILE, lanes), 0)
        col = lax.rem(lax.broadcasted_iota(jnp.int32, (TILE, lanes), 1), TILE)

        def group(i, carry):
            step = (i + 1) // 2
            y_ = lax.rem(y + 2 * NY + (HALF - step) * (2 * lax.rem(i, 2) - 1), NY)
            keys = kv[0, i].reshape(SLOTS * TILE, HD)
            values = kv[1, i].reshape(SLOTS * TILE, HD)
            if first:
                kv_t[0, i] = keys.T
                kv_t[1, i] = values.T
            query = q_bal[h0:h1, y_].reshape(lanes, HD)
            grad = g_in[h0:h1, y_].reshape(lanes, HD)
            scores = lax.dot_general(keys, query, nt, preferred_element_type=F32)
            dprobs = lax.dot_general(values, grad, nt, preferred_element_type=F32)
            parts = [scores[t * TILE : (t + 1) * TILE] for t in range(SLOTS)]
            parts[0] = jnp.where(row <= col, parts[0], FAR)
            bias = [jnp.concatenate([meta[y_, t : t + 1, :]] * n, axis=1) for t in range(SLOTS)]
            peaks = [jnp.max(parts[t], axis=0, keepdims=True) + bias[t] for t in range(SLOTS)]
            peak = functools.reduce(jnp.maximum, peaks)
            parts = [jnp.exp2((parts[t] - (peak - bias[t])) * (SCALE * LOG2E)) for t in range(SLOTS)]
            total = functools.reduce(jnp.add, [jnp.sum(part, axis=0, keepdims=True) for part in parts])
            inverse = 1.0 / total
            probs = jnp.concatenate([part * inverse for part in parts], axis=0)
            weights = probs.astype(BF16)
            delta = jnp.sum(probs * dprobs, axis=0, keepdims=True)
            dscores = (probs * (dprobs - delta)).astype(BF16)
            out_t = jnp.dot(kv_t[1, i], weights, preferred_element_type=F32)
            o_buf[h0:h1, y_] = out_t.T.astype(BF16).reshape(n, TILE, HD)
            dq_t = jnp.dot(kv_t[0, i], dscores, preferred_element_type=F32) * SCALE
            dq_bal[h0:h1, y_] = dq_t.T.astype(BF16).reshape(n, TILE, HD)
            dk = jnp.dot(dscores, query, preferred_element_type=F32).reshape(SLOTS, TILE, HD)
            dv = jnp.dot(weights, grad, preferred_element_type=F32).reshape(SLOTS, TILE, HD)
            if first:
                acc[0, i] = dk
                acc[1, i] = dv
            else:
                acc[0, i] += dk
                acc[1, i] += dv
            here = (y_ == y) & (own == c)
            for h in heads:
                cols = pl.ds(pl.multiple_of((6 * kv_head + 3 * c + h) * HD, HD), HD)
                move(o_buf.at[h, y_], out_ref.at[:, cols], o_ss.at[h], o_rs, dp_of(y_, own), here)
            if last:
                pair_out[i] = acc[other, i].astype(BF16)
                part = i // PART
                pltpu.make_async_remote_copy(
                    pair_out.at[i], pair_in.at[i], pc_ss.at[part], pc_rs.at[part],
                    device_id=(mate, z), device_id_type=MESH,
                ).start()
            return carry

        for h in heads:
            wait(q_raw.at[h], q_rs.at[h])

            def write_q(y_, at, value, h=h):
                q_bal[h, y_, at, :] = value

            place(lambda y_, at, h=h: q_raw[h, y_, at, :].astype(F32), write_q, (0, 1, 2))
        for h in heads:
            wait(g_in.at[h], g_rs.at[h])
        if not last:
            key_step(SLOTS - 1, 0)

            def piece(part, carry):
                @pl.when(part < PARTS - 1)
                def _():
                    key_step(SLOTS - 1, part + 1)

                for t in range(SLOTS):

                    @pl.when(z >= t)
                    def _():
                        wait(kv.at[0, pl.ds(part * PART, PART), t], kc_rs.at[t, part])

                for i in range(PART):
                    group(part * PART + i, carry)
                return carry

            lax.fori_loop(0, PARTS, piece, 0)
            return

        def some(part, carry):
            for i in range(PART):
                group(part * PART + i, carry)

            @pl.when(part > 0)
            def _():
                chain_begin(part - 1)

            return carry

        lax.fori_loop(0, PARTS, some, 0)

    def send_dq(heads):
        for h in heads:

            def write_dq(y_, at, value, h=h):
                dq_buf[h, y_, at, :] = value

            place(lambda y_, at, h=h: dq_bal[h, y_, at, :].astype(F32), write_dq, (2, 1, 0))
            cols = pl.ds(pl.multiple_of((6 * kv_head + 3 * c + h) * HD, HD), HD)
            for i in ORDER:
                to = lax.rem(y + i, NY)
                here = (to == y) & (own == c)
                move(dq_buf.at[h, to], dq_ref.at[:, cols], dq_ss.at[h], dq_rs, dp_of(to, own), here)

    attend((0, 1), True, False)
    send_dq((0, 1))

    def chain_step(t, part, cut):
        tiles, rows = pl.ds(part * PART, PART), pl.ds(cut * CUT, CUT)

        @pl.when(z >= t)
        def _():
            if t < SLOTS - 1:

                @pl.when(z < NZ - 1)
                def _():
                    wait(chain_in.at[t, tiles, rows], cz_rs.at[t, part, cut])

            total = acc[c, tiles, t, rows] + pair_in[tiles, t, rows].astype(F32)
            if t < SLOTS - 1:
                total = total + chain_in[t, tiles, rows].astype(F32)
            chain_out[t - 1, tiles, rows] = total.astype(BF16)
            pltpu.make_async_remote_copy(
                chain_out.at[t - 1, tiles, rows], chain_in.at[t - 1, tiles, rows],
                cz_ss.at[t - 1, part, cut], cz_rs.at[t - 1, part, cut],
                device_id=(dp, z - 1), device_id_type=MESH,
            ).start()

    def chain_begin(part):
        wait(pair_in.at[pl.ds(part * PART, PART)], pc_rs.at[part])
        for cut in range(2):
            chain_step(SLOTS - 1, part, cut)

    attend((2,), False, True)
    chain_begin(PARTS - 1)
    send_dq((2,))
    for t in reversed(range(1, SLOTS - 1)):

        for cut in range(2):

            def step(part, carry, t=t, cut=cut):
                chain_step(t, part, cut)
                return carry

            lax.fori_loop(0, PARTS, step, 0)


    factor = jnp.where(c == 0, SCALE, 1.0).astype(F32)

    def read_total(y_, at):
        i = turn(y_)
        total = acc[c, i, 0, at, :] + pair_in[i, 0, at, :].astype(F32) + chain_in[0, i, at, :].astype(F32)
        return total * factor

    def write_total(y_, at, value):
        fin[y_, at, :] = value

    cols = pl.ds(pl.multiple_of(kv_head * HD, HD), HD)
    for cut in range(2):
        rows = pl.ds(cut * CUT, CUT)

        @pl.when(z < NZ - 1)
        def _():
            for part in range(PARTS):
                wait(chain_in.at[0, part * PART : (part + 1) * PART, rows], cz_rs.at[0, part, cut])

        place(read_total, write_total, (2, 1, 0), cut * CUT, CUT)
        for i in ORDER:
            to = lax.rem(y + i, NY)
            here = (to == y) & (own == c)

            @pl.when(c == 0)
            def _():
                move(fin.at[to, rows], dk_ref.at[rows, cols], f_ss.at[cut], f_rs.at[0], dp_of(to, own), here)

            @pl.when(c == 1)
            def _():
                move(fin.at[to, rows], dv_ref.at[rows, cols], f_ss.at[cut], f_rs.at[1], dp_of(to, own), here)

    wait(out_ref, o_rs)
    wait(dq_ref, dq_rs)
    wait(dk_ref, f_rs.at[0])
    wait(dv_ref, f_rs.at[1])
    wait_sent(meta, meta_ss)
    wait_sent(kv_raw, kv_ss)
    for cut in range(2):
        wait_sent(fin.at[:, cut * CUT : (cut + 1) * CUT], f_ss.at[cut])
    for h in range(NH):
        wait_sent(q_raw.at[h], q_ss.at[h])
        wait_sent(g_in.at[h], g_ss.at[h])
        wait_sent(o_buf.at[h], o_ss.at[h])
        wait_sent(dq_buf.at[h], dq_ss.at[h])
    for part in range(PARTS):
        tiles = pl.ds(part * PART, PART)
        for t in range(SLOTS):

            @pl.when(z >= t)
            def _():
                wait(kv.at[0, tiles, t], kc_ss.at[t, part])

        for t in range(SLOTS - 1):

            @pl.when((z >= t) & (z < NZ - 1))
            def _():
                wait(kv.at[0, tiles, t], kz_ss.at[t, part])

    for part in range(PARTS):
        tiles = pl.ds(part * PART, PART)
        wait(pair_out.at[tiles], pc_ss.at[part])
        for t in range(SLOTS - 1):

            @pl.when(z >= t + 1)
            def _():
                for cut in range(2):
                    wait(chain_out.at[t, tiles, cut * CUT : (cut + 1) * CUT], cz_ss.at[t, part, cut])


def hand_over(*refs):
    copies = [pltpu.make_async_copy(refs[i], refs[4 + i], refs[8].at[i]) for i in range(4)]
    for copy in copies:
        copy.start()
    for copy in copies:
        copy.wait()


def on_device(q_in, k_in, v_in, dout, swap_plan, doc_ids):
    tile = (TILE, HD)
    dma = pltpu.SemaphoreType.DMA
    hbm, smem = pl.BlockSpec(memory_space=pl.ANY), pl.BlockSpec(memory_space=pltpu.SMEM)
    results = pl.pallas_call(
        kernel,
        out_shape=[pltpu.VMEM(a.shape, BF16) for a in (dout, q_in, k_in, v_in)],
        in_specs=[smem, smem, hbm, hbm, hbm, hbm],
        out_specs=[hbm] * 4,
        scratch_shapes=[
            pltpu.VMEM((8, HD), F32),
            pltpu.VMEM((NY, 8, HD), F32),
            pltpu.VMEM((NY, *tile), BF16),
            pltpu.VMEM((2, NY, SLOTS, *tile), BF16),
            pltpu.VMEM((2, NY, HD, SLOTS * TILE), BF16),
            pltpu.VMEM((NH, NY, *tile), BF16),
            pltpu.VMEM((NH, NY, *tile), BF16),
            pltpu.VMEM((NH, NY, *tile), BF16),
            pltpu.VMEM((NH, NY, *tile), BF16),
            pltpu.VMEM((NH, NY, *tile), BF16),
            pltpu.VMEM((NH, NY, *tile), BF16),
            pltpu.VMEM((2, NY, SLOTS, *tile), F32),
            pltpu.VMEM((NY, SLOTS, *tile), BF16),
            pltpu.VMEM((NY, SLOTS, *tile), BF16),
            pltpu.VMEM((SLOTS - 1, NY, *tile), BF16),
            pltpu.VMEM((SLOTS - 1, NY, *tile), BF16),
            pltpu.VMEM((NY, *tile), BF16),
            dma, dma, dma, dma,
            dma((NH,)), dma((NH,)), dma((NH,)), dma((NH,)),
            dma((SLOTS - 1, PARTS)), dma((SLOTS - 1, PARTS)), dma((SLOTS, PARTS)), dma((SLOTS, PARTS)),
            dma((NH,)), dma, dma((NH,)), dma,
            dma((PARTS,)), dma((PARTS,)), dma((SLOTS - 1, PARTS, 2)), dma((SLOTS - 1, PARTS, 2)),
            dma((2,)), dma((2,)),
        ],
        compiler_params=pltpu.CompilerParams(
            collective_id=0, has_side_effects=True, vmem_limit_bytes=62 << 20
        ),
    )(swap_plan.reshape(1, 3), doc_ids, q_in, k_in, v_in, dout)
    return pl.pallas_call(
        hand_over,
        out_shape=[jax.ShapeDtypeStruct(a.shape, BF16) for a in results],
        in_specs=[pl.BlockSpec(memory_space=pltpu.VMEM)] * 4,
        out_specs=[hbm] * 4,
        scratch_shapes=[dma((4,))],
        compiler_params=pltpu.CompilerParams(vmem_limit_bytes=1 << 20),
    )(*[pltpu.with_memory_space_constraint(a, pltpu.VMEM) for a in results])


def solution(mesh):
    rows = P(("dp", "head"), None)
    return jax.shard_map(
        on_device,
        mesh=mesh,
        in_specs=(rows, rows, rows, rows, P(None, ("dp", "head")), P("dp", None)),
        out_specs=(rows, rows, rows, rows),
        check_vma=False,
    )
```
